32 devices in a mesh: ctx: 16 (over z, y, x), head: 2 (over core).
Axes of the slice: x: 2, y: 2, z: 4, core: 2. Of those that a mesh axis runs over, the one named last changes fastest.
Arguments:
- lin_queries: bfloat16 [4096, 8192], P('ctx', 'head'), may hold values from -6 to 6
- lin_keys: bfloat16 [4096, 8192], P('ctx', 'head'), may hold values from -6 to 6
- lin_values: bfloat16 [4096, 8192], P('ctx', 'head'), may hold values from -21 to 21
- log_decay: float32 [4096, 64], P('ctx', 'head'), may hold values from -1 to 0
- lin_gate: bfloat16 [4096, 8192], P('ctx', 'head'), may hold values from -6 to 6
- norm_gain: float32 [8192], P('head'), may hold values from 0.1 to 1.9
- soft_queries: bfloat16 [4096, 8192], P('ctx', 'head'), may hold values from -6 to 6
- slab_keys: bfloat16 [4096, 1024], P('ctx', 'head'), may hold values from -6 to 6
- slab_values: bfloat16 [4096, 1024], P('ctx', 'head'), may hold values from -6 to 6
- cache_keys: bfloat16 [16384, 1024], P('ctx', 'head'), may hold values from -6 to 6
- cache_values: bfloat16 [16384, 1024], P('ctx', 'head'), may hold values from -6 to 6
- block_lists: int32 [32, 16], replicated, may hold values from 0 to 127, as said below
- live_counts: int32 [32], replicated, may hold values from 2 to 16
Outputs:
- lin_out: bfloat16 [4096, 8192], P('ctx', 'head')
- soft_out: bfloat16 [4096, 8192], P('ctx', 'head')
The draws below stay inside these ranges and needn't reach their ends.
Inputs may be any that keep to these rules, and one draw needn't show every extreme that they name: `block_lists`: cache block g lies on ctx index g // 8. One list names 16 blocks on 16 different ctx indices, and all lists of the 2 query blocks of one ctx index name at most one block of any one ctx index. Entries from live_counts on are not read.
All inputs are finite; a program needn't handle non-finite values.
Results may differ from the reference program's by a relative error of at most 0.0046.
Values may be sent and summed in bfloat16 or wider, within the bound.
No kernel may reach another device: no remote copies, remote signals or barrier semaphores. Data moves between devices by JAX's collectives and lax.ppermute only.
A program may use at most 192 MiB of HBM per device.

```python
import jax
import jax.numpy as jnp
from jax import lax

QUERY_HEADS = 64
KV_HEADS = 8
HD = 128
TOK_DEV = 256
BLOCK = 128
NSEL = 16
SLAB_TOKENS = 4096
CACHE = 16384
QB_DEV = 2
BLK_DEV = 8
QBLOCKS = 32
CBLOCKS = 128
RSET = 16
QF = 8192
KF = 1024


def draw_lin_values(key, part):
    head_place = (jnp.arange(QF) // HD).astype(jnp.float32) / max(QUERY_HEADS - 1, 1)
    base = jnp.clip(jax.random.normal(jax.random.fold_in(key, 31), (SLAB_TOKENS, QF), jnp.float32), -6.0, 6.0)
    spread = 0.5 * jnp.log(3.0)
    head_scale = jnp.exp(spread * head_place)
    return (base * head_scale[None, :]).astype(jnp.bfloat16)


def draw_log_decay(key, part):
    fast_share = 0.5
    fast = jax.random.uniform(jax.random.fold_in(key, 41), (QUERY_HEADS,), jnp.float32) < fast_share
    slow_rate = jnp.exp(jax.random.uniform(jax.random.fold_in(key, 42), (QUERY_HEADS,), jnp.float32, jnp.log(0.1), jnp.log(0.5))) / SLAB_TOKENS
    fast_rate = jax.random.uniform(jax.random.fold_in(key, 43), (QUERY_HEADS,), jnp.float32, 1.0 / 50.0, 1.0 / 30.0)
    rate = jnp.where(fast, fast_rate, slow_rate)
    segments = SLAB_TOKENS // TOK_DEV
    seg_factor = jnp.exp(jax.random.uniform(jax.random.fold_in(key, 44), (segments, QUERY_HEADS), jnp.float32, jnp.log(0.6), jnp.log(1.5)))
    jitter = jax.random.uniform(jax.random.fold_in(key, 45), (SLAB_TOKENS, QUERY_HEADS), jnp.float32, 0.5, 1.5)
    steady_level = -rate[None, :] * seg_factor[jnp.arange(SLAB_TOKENS) // TOK_DEV] * jitter
    spike_position = jax.random.randint(jax.random.fold_in(key, 46), (2, QUERY_HEADS), 0, SLAB_TOKENS)
    layer_depth = jax.random.uniform(jax.random.fold_in(key, 47), (2, QUERY_HEADS), jnp.float32, 0.22, 0.69)
    device_positions = jnp.arange(SLAB_TOKENS)[:, None]
    spike_events = jnp.where(device_positions == spike_position[0][None, :], layer_depth[0][None, :], 0.0) + jnp.where(device_positions == spike_position[1][None, :], layer_depth[1][None, :], 0.0)
    return (steady_level - spike_events).astype(jnp.float32)


def draw_soft_queries(key, part):
    base = jnp.clip(jax.random.normal(jax.random.fold_in(key, 51), (SLAB_TOKENS, QF), jnp.float32), -6.0, 6.0)
    return base.astype(jnp.bfloat16)


def draw_cache_keys(key, part):
    base = jnp.clip(jax.random.normal(jax.random.fold_in(key, 61), (CACHE, KF), jnp.float32), -6.0, 6.0)
    return base.astype(jnp.bfloat16)


def request_sets(base_key, device_count):
    hotness = jax.random.randint(jax.random.fold_in(base_key, 11), (device_count,), 0, 5)
    noise = jax.random.randint(jax.random.fold_in(base_key, 12), (device_count, device_count), 0, 65536)
    owner_ids = jnp.arange(device_count, dtype=jnp.int32)
    scores = (hotness[None, :] * 24576 + noise) * device_count + owner_ids[None, :]
    unused, owners = lax.top_k(scores, RSET)
    spots = jax.random.randint(jax.random.fold_in(base_key, 13), (device_count, RSET), 0, BLK_DEV)
    return (owners * BLK_DEV + spots).astype(jnp.int32)


def draw_block_lists(key, part):
    device_count = QBLOCKS // QB_DEV
    choices_all = request_sets(key, device_count)
    picker = jax.random.randint(jax.random.fold_in(key, 14), (QBLOCKS, RSET), 0, 65536)
    picker = picker * RSET + jnp.arange(RSET, dtype=jnp.int32)[None, :]
    unused, chosen = lax.top_k(picker, NSEL)
    own_sets = choices_all[jnp.arange(QBLOCKS) // QB_DEV]
    return jnp.take_along_axis(own_sets, chosen, axis=1).astype(jnp.int32)


def draw_live_counts(key, part):
    device_count = QBLOCKS // QB_DEV
    heavy = jax.random.randint(jax.random.fold_in(key, 21), (device_count,), 0, 8) == 0
    light = jax.random.randint(jax.random.fold_in(key, 22), (device_count,), 1, 3) * (NSEL // 4)
    levels = jnp.where(heavy, NSEL, light)
    trimmed = jax.random.randint(jax.random.fold_in(key, 23), (QBLOCKS,), 0, 2) * (NSEL // 8)
    counts_all = jnp.maximum(1, levels[jnp.arange(QBLOCKS) // QB_DEV] - trimmed)
    forced = jax.random.randint(jax.random.fold_in(key, 24), (), 0, QBLOCKS)
    counts_all = jnp.where(jnp.arange(QBLOCKS) == forced, NSEL, counts_all)
    return counts_all.astype(jnp.int32)


def block_levels(stream_key, extent, cuts, low, top_value):
    def one(dim, blocks):
        steps = jax.random.uniform(jax.random.fold_in(jax.random.fold_in(stream_key, 6), dim), (blocks,), jnp.float32, low / len(cuts), top_value / len(cuts))
        return jnp.repeat(jnp.exp(steps), extent[dim] // blocks).reshape((-1,) + (1,) * (len(extent) - dim - 1))

    gain = one(*cuts[0])
    for cut in cuts[1:]:
        gain = gain * one(*cut)
    return gain


def centred(key, shape, scale, bound, cuts=(), kind=jnp.bfloat16):
    array = jax.random.normal(key, shape, jnp.float32) * scale
    if len(cuts) > 0:
        array = block_levels(key, shape, cuts, -0.22, 0.18) * array
    return jnp.clip(array, min=-bound, max=bound).astype(kind)


def setup_inputs(seed: int = 0) -> dict:
    key_list = jax.random.split(jax.random.key(seed), 14)
    lin_queries = centred(key_list[0], (SLAB_TOKENS, QF), 1.0, 6.0, ((0, 16), (1, 2)))
    lin_keys = centred(key_list[1], (SLAB_TOKENS, QF), 1.0, 6.0, ((0, 16), (1, 2)))
    lin_values = draw_lin_values(jax.random.fold_in(key_list[13], 71), 0)
    log_decay = draw_log_decay(jax.random.fold_in(key_list[13], 71), 0)
    lin_gate = centred(key_list[4], (SLAB_TOKENS, QF), 1.0, 6.0, ((0, 16), (1, 2)))
    norm_gain = jnp.clip(1.0 + 0.18 * jax.random.normal(key_list[5], (QF,), jnp.float32), 0.1, 1.9)
    soft_queries = draw_soft_queries(jax.random.fold_in(key_list[13], 71), 0)
    slab_keys = centred(key_list[7], (SLAB_TOKENS, KF), 1.0, 6.0, ((0, 16), (1, 2)))
    slab_values = centred(key_list[8], (SLAB_TOKENS, KF), 1.0, 6.0, ((0, 16), (1, 2)))
    cache_keys = draw_cache_keys(jax.random.fold_in(key_list[13], 71), 0)
    cache_values = centred(key_list[10], (CACHE, KF), 1.0, 6.0, ((0, 16), (1, 2)))
    block_lists = draw_block_lists(jax.random.fold_in(key_list[13], 71), 0)
    live_counts = draw_live_counts(jax.random.fold_in(key_list[13], 71), 0)
    return {"lin_queries": lin_queries, "lin_keys": lin_keys, "lin_values": lin_values, "log_decay": log_decay, "lin_gate": lin_gate, "norm_gain": norm_gain, "soft_queries": soft_queries, "slab_keys": slab_keys, "slab_values": slab_values, "cache_keys": cache_keys, "cache_values": cache_values, "block_lists": block_lists, "live_counts": live_counts}


def lightning_part(lin_queries, lin_keys, lin_values, log_decay, lin_gate, norm_gain):
    segments = SLAB_TOKENS // TOK_DEV
    act_queries = jax.nn.silu(lin_queries.astype(jnp.float32)).astype(jnp.bfloat16)
    act_keys = jax.nn.silu(lin_keys.astype(jnp.float32)).astype(jnp.bfloat16)
    act_queries = act_queries.reshape(segments, TOK_DEV, QUERY_HEADS, HD)
    act_keys = act_keys.reshape(segments, TOK_DEV, QUERY_HEADS, HD)
    values_all = lin_values.reshape(segments, TOK_DEV, QUERY_HEADS, HD)
    decays = log_decay.reshape(segments, TOK_DEV, QUERY_HEADS)
    causal = jnp.arange(TOK_DEV)[:, None] >= jnp.arange(TOK_DEV)[None, :]

    def segment_step(entering, pieces):
        seg_queries, seg_keys, seg_values, seg_decay = pieces
        running = jnp.cumsum(seg_decay, axis=0)
        seg_total = running[-1]
        flipped = running.T
        gaps = flipped[:, :, None] - flipped[:, None, :]
        weight = jnp.where(causal[None], jnp.exp(jnp.minimum(gaps, 0.0)), 0.0)
        scores = jnp.einsum('thd,shd->hts', seg_queries.astype(jnp.float32), seg_keys.astype(jnp.float32))
        lin_scores = (scores * weight).astype(jnp.bfloat16)
        intra = jnp.einsum('hts,shd->thd', lin_scores.astype(jnp.float32), seg_values.astype(jnp.float32))
        inter = jnp.exp(running)[:, :, None] * jnp.einsum('thd,hde->the', seg_queries.astype(jnp.float32), entering, precision=lax.Precision.HIGHEST)
        fade = jnp.exp(seg_total[None, :] - running)
        seg_state = jnp.einsum('shd,she->hde', seg_keys.astype(jnp.float32) * fade[:, :, None], seg_values.astype(jnp.float32), precision=lax.Precision.HIGHEST)
        leaving = jnp.exp(seg_total)[:, None, None] * entering + seg_state
        return (leaving, intra + inter)
    start_state = jnp.zeros((QUERY_HEADS, HD, HD), jnp.float32)
    unused, lin_attn = lax.scan(segment_step, start_state, (act_queries, act_keys, values_all, decays))
    lin_attn = lin_attn.reshape(SLAB_TOKENS, QUERY_HEADS * HD)
    squares = lax.optimization_barrier(jnp.mean(lin_attn * lin_attn, axis=1))
    scaling = lax.rsqrt(squares + 1e-06)
    gated = lin_attn * scaling[:, None] * norm_gain[None, :] * jax.nn.sigmoid(lin_gate.astype(jnp.float32))
    return gated.astype(jnp.bfloat16)

def softmax_part(soft_queries, slab_keys, slab_values, cache_keys, cache_values, block_lists, live_counts):
    group_size = QUERY_HEADS // KV_HEADS
    cache_key_blocks = cache_keys.reshape(CBLOCKS, BLOCK, KV_HEADS, HD)
    cache_value_blocks = cache_values.reshape(CBLOCKS, BLOCK, KV_HEADS, HD)
    inverse_root = 1.0 / HD ** 0.5

    def one_block(block_index):
        listed = block_lists[block_index]
        live_count = live_counts[block_index]
        chosen_keys = cache_key_blocks[listed].reshape(NSEL * BLOCK, KV_HEADS, HD)
        chosen_values = cache_value_blocks[listed].reshape(NSEL * BLOCK, KV_HEADS, HD)
        seg_start = (block_index // QB_DEV * TOK_DEV).astype(jnp.int32)
        own_keys = lax.dynamic_slice_in_dim(slab_keys, seg_start, TOK_DEV, 0).reshape(TOK_DEV, KV_HEADS, HD)
        own_values = lax.dynamic_slice_in_dim(slab_values, seg_start, TOK_DEV, 0).reshape(TOK_DEV, KV_HEADS, HD)
        query_start = (block_index * BLOCK).astype(jnp.int32)
        queries = lax.dynamic_slice_in_dim(soft_queries, query_start, BLOCK, 0).reshape(BLOCK, KV_HEADS, group_size, HD)
        all_keys = jnp.concatenate([chosen_keys, own_keys], axis=0).astype(jnp.float32)
        all_values = jnp.concatenate([chosen_values, own_values], axis=0).astype(jnp.float32)
        scores = jnp.einsum('tkgd,skd->kgts', queries.astype(jnp.float32), all_keys) * inverse_root
        cache_live = jnp.arange(NSEL * BLOCK) // BLOCK < live_count
        positions = block_index % QB_DEV * BLOCK + jnp.arange(BLOCK)
        causal = jnp.arange(TOK_DEV)[None, :] <= positions[:, None]
        allowed = jnp.concatenate([jnp.broadcast_to(cache_live[None, :], (BLOCK, NSEL * BLOCK)), causal], axis=1)
        scores = jnp.where(allowed[None, None], scores, -1e+30)
        highest = lax.optimization_barrier(jnp.max(scores, axis=3, keepdims=True))
        weights = jnp.exp(scores - highest)
        totals = lax.optimization_barrier(jnp.sum(weights, axis=3))
        soft_weights = weights.astype(jnp.bfloat16)
        mixed = jnp.einsum('kgts,skd->tkgd', soft_weights.astype(jnp.float32), all_values)
        normed = mixed / jnp.transpose(totals, (2, 0, 1))[:, :, :, None]
        return normed.astype(jnp.bfloat16).reshape(BLOCK, QUERY_HEADS * HD)
    outputs = lax.map(one_block, jnp.arange(QBLOCKS, dtype=jnp.int32))
    return outputs.reshape(SLAB_TOKENS, QUERY_HEADS * HD)

def reference(lin_queries, lin_keys, lin_values, log_decay, lin_gate, norm_gain, soft_queries, slab_keys, slab_values, cache_keys, cache_values, block_lists, live_counts):
    lin_out = lightning_part(lin_queries, lin_keys, lin_values, log_decay, lin_gate, norm_gain)
    soft_out = softmax_part(soft_queries, slab_keys, slab_values, cache_keys, cache_values, block_lists, live_counts)
    return (lin_out, soft_out)
```

```python
import functools
import math

import jax
import jax.numpy as jnp
from jax import lax
from jax.experimental import pallas as pl
from jax.experimental.pallas import tpu as pltpu
from jax.sharding import PartitionSpec as P

HD = 128
BLOCK = 128
STEP_HEADS = 8
PAD = 16
VMEM_LIMIT = 56 * 1024 * 1024
F32 = jnp.float32
BF16 = jnp.bfloat16
NT = (((1,), (1,)), ((), ()))
TN = (((0,), (0,)), ((), ()))


def params(**more):
    return pltpu.CompilerParams(vmem_limit_bytes=VMEM_LIMIT, **more)


def cost(microseconds):
    return pl.CostEstimate(
        flops=0, bytes_accessed=int(microseconds * 3.69e6), transcendentals=0
    )


def silu(u):
    half = u.astype(F32) * 0.5
    return (half + half * jnp.tanh(half)).astype(BF16)


def pack_kernel(first, spots, keys, values, *rest):
    outs, sems = rest[:-1], rest[-1]
    copies = []
    start = first
    for part, out in enumerate(outs):
        width = out.shape[3]
        for dest in range(out.shape[0]):
            rows = pl.ds(pl.multiple_of(spots[dest] * BLOCK, BLOCK), BLOCK)
            for kind, source in enumerate((keys, values)):
                copies.append(
                    pltpu.make_async_copy(
                        source.at[rows, pl.ds(start, width)],
                        out.at[dest, kind],
                        sems.at[part, dest, kind],
                    )
                )
        start += width
    for copy in copies:
        copy.start()
    for copy in copies:
        copy.wait()


def pack(spots, keys, values, first, widths):
    n = spots.shape[0]
    whole = pl.BlockSpec(keys.shape, lambda i, _: (0, 0))
    return pl.pallas_call(
        functools.partial(pack_kernel, first),
        out_shape=[jax.ShapeDtypeStruct((n, 2, BLOCK, width), BF16) for width in widths],
        grid_spec=pltpu.PrefetchScalarGridSpec(
            num_scalar_prefetch=1,
            grid=(1,),
            in_specs=[whole, whole],
            out_specs=[pl.BlockSpec(memory_space=pl.ANY)] * len(widths),
            scratch_shapes=[pltpu.SemaphoreType.DMA((len(widths), n, 2))],
        ),
        compiler_params=params(),
        cost_estimate=cost(4),
        name="pack",
    )(spots, keys, values)


def state_kernel(group, place, keys, values, decay, running_out, *rest):
    outs, running, hold = rest[:group], rest[group], rest[group + 1]
    step = pl.program_id(0)
    rows = keys.shape[0]
    mine = place[0]
    per = hold.shape[1] // HD

    @pl.when(step == 0)
    def _():
        s = lax.broadcasted_iota(jnp.int32, (rows, rows), 0)
        t = lax.broadcasted_iota(jnp.int32, (rows, rows), 1)
        running[...] = lax.dot_general(
            decay[...],
            (s <= t).astype(F32),
            TN,
            precision=lax.Precision.HIGHEST,
            preferred_element_type=F32,
        )

    here = running[pl.ds(pl.multiple_of(step * STEP_HEADS, STEP_HEADS), STEP_HEADS), :]
    running_out[...] = here
    total = here[:, rows - 1 : rows]
    fade = jnp.exp(total - here)
    wide = jnp.broadcast_to(total, (STEP_HEADS, HD))
    high = wide.astype(BF16).astype(F32)
    middle = (wide - high).astype(BF16).astype(F32)
    low = wide - high - middle
    for dest in range(STEP_HEADS // per):
        slot = (step * (STEP_HEADS // per) + dest) ^ mine
        for i in range(per):
            head = dest * per + i
            columns = slice(head * HD, (head + 1) * HD)
            act = silu(keys[:, columns]).T
            state = jnp.dot(
                (act.astype(F32) * fade[head : head + 1, :]).astype(BF16),
                values[:, columns],
                preferred_element_type=F32,
            )
            hold[slot, i * HD : (i + 1) * HD, :] = state.astype(BF16)
        mine_rows = slice(dest * per, (dest + 1) * per)
        tail = [high[mine_rows], middle[mine_rows], low[mine_rows]]
        if 3 * per < PAD:
            tail.append(jnp.zeros((PAD - 3 * per, HD), F32))
        hold[slot, per * HD :, :] = jnp.concatenate(tail, axis=0).astype(BF16)

    @pl.when(step == pl.num_programs(0) - 1)
    def _():
        for k, out in enumerate(outs):
            out[...] = hold[k]


def segment_states(keys, values, decay, place, group):
    rows, heads = decay.shape
    per = heads // group
    size = per * HD + PAD
    wide = STEP_HEADS * HD
    return pl.pallas_call(
        functools.partial(state_kernel, group),
        out_shape=[jax.ShapeDtypeStruct((heads, rows), F32)]
        + [jax.ShapeDtypeStruct((size, HD), BF16)] * group,
        grid_spec=pltpu.PrefetchScalarGridSpec(
            num_scalar_prefetch=1,
            grid=(heads // STEP_HEADS,),
            in_specs=[
                pl.BlockSpec((rows, wide), lambda i, _: (0, i)),
                pl.BlockSpec((rows, wide), lambda i, _: (0, i)),
                pl.BlockSpec((rows, heads), lambda i, _: (0, 0)),
            ],
            out_specs=[pl.BlockSpec((STEP_HEADS, rows), lambda i, _: (i, 0))]
            + [pl.BlockSpec((size, HD), lambda i, _: (0, 0))] * group,
            scratch_shapes=[pltpu.VMEM((heads, rows), F32), pltpu.VMEM((group, size, HD), BF16)],
        ),
        compiler_params=params(),
        cost_estimate=cost(6),
        name="segment_states",
    )(place, keys, values, decay)


def intra_kernel(queries, keys, values, running, out):
    rows = queries.shape[0]
    column = running[...].T
    t = lax.broadcasted_iota(jnp.int32, (BLOCK, BLOCK), 0)
    s = lax.broadcasted_iota(jnp.int32, (BLOCK, BLOCK), 1)
    causal = s <= t
    for head in range(STEP_HEADS):
        columns = slice(head * HD, (head + 1) * HD)
        act_q = silu(queries[:, columns])
        act_k = silu(keys[:, columns])
        v = values[:, columns]
        for a in range(rows // BLOCK):
            mine = slice(a * BLOCK, (a + 1) * BLOCK)
            seen = (a + 1) * BLOCK
            scores = lax.dot_general(act_q[mine], act_k[:seen], NT, preferred_element_type=F32)
            gaps = column[mine, head : head + 1] - running[head : head + 1, :seen]
            pieces = []
            for b in range(a + 1):
                part = slice(b * BLOCK, (b + 1) * BLOCK)
                gap = jnp.minimum(gaps[:, part], 0.0)
                if b == a:
                    gap = jnp.where(causal, gap, -1e30)
                pieces.append((scores[:, part] * jnp.exp(gap)).astype(BF16))
            weights = pieces[0] if a == 0 else jnp.concatenate(pieces, axis=1)
            out[mine, columns] = jnp.dot(weights, v[:seen], preferred_element_type=F32)


def intra(queries, keys, values, running):
    rows, features = queries.shape
    wide = STEP_HEADS * HD
    block = pl.BlockSpec((rows, wide), lambda i: (0, i))
    return pl.pallas_call(
        intra_kernel,
        out_shape=jax.ShapeDtypeStruct((rows, features), F32),
        grid=(features // wide,),
        in_specs=[block, block, block, pl.BlockSpec((STEP_HEADS, rows), lambda i: (i, 0))],
        out_specs=block,
        compiler_params=params(),
        cost_estimate=cost(10),
        name="intra",
    )(queries, keys, values, running)


def read_total(message, per, head):
    base = per * HD + head
    rows = [message[base + k * per : base + k * per + 1, :].astype(F32) for k in range(3)]
    return rows[0] + rows[1] + rows[2]


def walk_kernel(group, per, with_start, place, *refs):
    arrived = refs[:group]
    mine = place[0]
    if with_start:
        start, outs, hold = refs[group], refs[group + 1 : -1], refs[-1]
    else:
        outs, hold = refs[group:-1], refs[-1]
    for k in range(group):
        hold[mine ^ k] = arrived[k][...]
    for head in range(per):
        rows = slice(head * HD, (head + 1) * HD)
        if with_start:
            state = start[rows, :].astype(F32)
        else:
            state = jnp.zeros((HD, HD), F32)
        for j in range(group):
            message = hold.at[j]
            own = message[rows, :].astype(F32)
            fade = jnp.exp(read_total(message[...], per, head))
            if with_start:
                hold[j, rows, :] = state.astype(BF16)
            state = fade * state + own
        if not with_start:
            outs[0][rows, :] = state.astype(outs[0].dtype)
    if with_start:
        for k in range(group):
            outs[k][...] = hold[mine ^ k, : per * HD, :]


def walk(arrived, place, start=None):
    group = len(arrived)
    size = arrived[0].shape[0]
    per = (size - PAD) // HD
    whole = pl.BlockSpec((size, HD), lambda i, _: (0, 0))
    part = pl.BlockSpec((per * HD, HD), lambda i, _: (0, 0))
    with_start = start is not None
    outs = group if with_start else 1
    return pl.pallas_call(
        functools.partial(walk_kernel, group, per, with_start),
        out_shape=[jax.ShapeDtypeStruct((per * HD, HD), BF16)] * outs,
        grid_spec=pltpu.PrefetchScalarGridSpec(
            num_scalar_prefetch=1,
            grid=(1,),
            in_specs=[whole] * group + [part] * with_start,
            out_specs=[part] * outs,
            scratch_shapes=[pltpu.VMEM((group, size, HD), BF16)],
        ),
        compiler_params=params(),
        cost_estimate=cost(2.5),
        name="walk_states",
    )(place, *arrived, *((start,) if with_start else ()))


def join_kernel(group, place, queries, inside, running, *refs):
    states, (out, squares), (hold, total) = refs[:group], refs[group : group + 2], refs[group + 2 :]
    step = pl.program_id(0)
    mine = place[0]
    per = hold.shape[1] // HD

    @pl.when(step == 0)
    def _():
        for k in range(group):
            hold[mine ^ k] = states[k][...]
        total[...] = jnp.zeros_like(total)

    grow = jnp.exp(running[...].T)
    summed = jnp.zeros(total.shape, F32)
    for head in range(STEP_HEADS):
        columns = slice(head * HD, (head + 1) * HD)
        owner = step * (STEP_HEADS // per) + head // per
        part = (head % per) * HD
        passed = jnp.dot(
            silu(queries[:, columns]), hold[owner, part : part + HD, :], preferred_element_type=F32
        )
        attn = inside[:, columns] + grow[:, head : head + 1] * passed
        out[:, columns] = attn
        summed += attn * attn
    total[...] += summed

    @pl.when(step == pl.num_programs(0) - 1)
    def _():
        squares[...] = lax.dot_general(
            jnp.ones((8, HD), F32),
            total[...],
            NT,
            precision=lax.Precision.HIGHEST,
            preferred_element_type=F32,
        )


def join(queries, inside, running, states, place):
    rows, features = queries.shape
    wide = STEP_HEADS * HD
    block = pl.BlockSpec((rows, wide), lambda i, _: (0, i))
    group = len(states)
    return pl.pallas_call(
        functools.partial(join_kernel, group),
        out_shape=[
            jax.ShapeDtypeStruct((rows, features), F32),
            jax.ShapeDtypeStruct((8, rows), F32),
        ],
        grid_spec=pltpu.PrefetchScalarGridSpec(
            num_scalar_prefetch=1,
            grid=(features // wide,),
            in_specs=[block, block, pl.BlockSpec((STEP_HEADS, rows), lambda i, _: (i, 0))]
            + [pl.BlockSpec(state.shape, lambda i, _: (0, 0)) for state in states],
            out_specs=[block, pl.BlockSpec((8, rows), lambda i, _: (0, 0))],
            scratch_shapes=[
                pltpu.VMEM((group,) + states[0].shape, BF16),
                pltpu.VMEM((rows, HD), F32),
            ],
        ),
        compiler_params=params(),
        cost_estimate=cost(7),
        name="join_states",
    )(place, queries, inside, running, *states)


def gate_kernel(features, attn, gate, gain, *refs):
    out = refs[-1]
    squares = refs[0][...]
    for more in refs[1:-1]:
        squares = squares + more[...]
    scaling = lax.rsqrt(squares / features + 1e-06).T[:, :1]
    half = gate[...].astype(F32) * 0.5
    opened = 0.5 + 0.5 * jnp.tanh(half)
    out[...] = (attn[...] * scaling * gain[...] * opened).astype(BF16)


def gated(attn, gate, gain, squares, features):
    rows, here = attn.shape
    wide = STEP_HEADS * HD
    block = pl.BlockSpec((rows, wide), lambda i: (0, i))
    return pl.pallas_call(
        functools.partial(gate_kernel, features),
        out_shape=jax.ShapeDtypeStruct((rows, here), BF16),
        grid=(here // wide,),
        in_specs=[block, block, pl.BlockSpec((1, wide), lambda i: (0, i))]
        + [pl.BlockSpec((8, rows), lambda i: (0, 0))] * len(squares),
        out_specs=block,
        compiler_params=params(),
        cost_estimate=cost(6),
        name="gated_norm",
    )(attn, gate, gain.reshape(1, here), *squares)


def exchange_in_group(messages, group):
    n = lax.axis_size("ctx")
    return [messages[0]] + [
        lax.ppermute(messages[k], "ctx", [(i, i ^ k) for i in range(n)]) for k in range(1, group)
    ]


def states_before_group(total, logs, group):
    n = lax.axis_size("ctx")
    groups = n // group

    def shift(array, by):
        return lax.ppermute(
            array, "ctx", [(i, i + by * group) for i in range(n - by * group)]
        )

    before = shift(total, 1)
    if groups == 2:
        return before
    span = shift(logs, 1)
    reach = 1
    while reach < groups - 1:
        far = shift(before, reach).astype(F32)
        before = (
            far * jnp.exp(span)[:, None] + before.astype(F32)
        ).astype(BF16)
        span = span + shift(span, reach)
        reach *= 2
    return before


def soft_kernel(
    chosen, owners, counts, queries, slab_k, slab_v, arrived, *refs
):
    out, scores, top, weight_sum, mixed = refs[-5:]
    b = pl.program_id(1)
    count = counts[b]
    heads = queries.shape[1] // HD
    chunk = 2 * BLOCK
    chunks = heads * BLOCK // chunk
    scale = math.log2(math.e) / math.sqrt(HD)
    low = -1e30

    def rows_of(r):
        return jnp.concatenate(
            [queries[:, (2 * r + i) * HD : (2 * r + i + 1) * HD] for i in range(2)], axis=0
        )

    def pair(kind, first, second):
        return jnp.concatenate(
            [
                arrived[owners[b * chosen + first], kind],
                arrived[owners[b * chosen + second], kind],
            ],
            axis=0,
        )

    def score(tile, k, allowed, first):
        for r in range(chunks):
            at = slice(r * chunk, (r + 1) * chunk)
            s = lax.dot_general(rows_of(r), k, NT, preferred_element_type=F32)
            if allowed is not None:
                s = jnp.where(allowed, s, low)
            scores[tile, at, :] = s
            here = jnp.maximum(s[:, :BLOCK], s[:, BLOCK:])
            top[at, :] = here if first else jnp.maximum(top[at, :], here)

    t = lax.broadcasted_iota(jnp.int32, (chunk, chunk), 0) % BLOCK
    s_at = lax.broadcasted_iota(jnp.int32, (chunk, chunk), 1)
    score(0, slab_k[...], s_at <= t + b * BLOCK, True)
    pairs = count // 2

    def score_pair(p, _):
        score(p + 1, pair(0, 2 * p, 2 * p + 1), None, False)
        return 0

    lax.fori_loop(0, pairs, score_pair, 0)
    odd = count % 2 == 1

    @pl.when(odd)
    def _():
        score(pairs + 1, pair(0, count - 1, count - 1), s_at < BLOCK, False)

    for r in range(chunks):
        at = slice(r * chunk, (r + 1) * chunk)
        highest = jnp.max(top[at, :], axis=1, keepdims=True) * scale
        top[at, :] = jnp.broadcast_to(highest, (chunk, BLOCK))

    def mix(tile, v, first):
        for r in range(chunks):
            at = slice(r * chunk, (r + 1) * chunk)
            highest = top[at, :]
            left = jnp.exp2(scores[tile, at, :BLOCK] * scale - highest)
            right = jnp.exp2(scores[tile, at, BLOCK:] * scale - highest)
            w = jnp.concatenate([left.astype(BF16), right.astype(BF16)], axis=1)
            more = jnp.dot(w, v, preferred_element_type=F32)
            if first:
                weight_sum[at, :] = left + right
                mixed[at, :] = more
            else:
                weight_sum[at, :] += left + right
                mixed[at, :] += more

    mix(0, slab_v[...], True)

    def mix_pair(p, _):
        mix(p + 1, pair(1, 2 * p, 2 * p + 1), False)
        return 0

    lax.fori_loop(0, pairs, mix_pair, 0)

    @pl.when(odd)
    def _():
        mix(pairs + 1, pair(1, count - 1, count - 1), False)

    for head in range(heads):
        at = slice(head * BLOCK, (head + 1) * BLOCK)
        total = jnp.sum(weight_sum[at, :], axis=1, keepdims=True)
        out[:, head * HD : (head + 1) * HD] = (mixed[at, :] / total).astype(BF16)


def soft_part(owners, counts, queries, slab_k, slab_v, arrived, first, chosen, so_far):
    rows, features = queries.shape
    kv_here = arrived.shape[3] // HD
    n = arrived.shape[0]
    wide = features // (slab_k.shape[1] // HD)
    blocks = rows // BLOCK
    grid_spec = pltpu.PrefetchScalarGridSpec(
        num_scalar_prefetch=2,
        grid=(kv_here, blocks),
        in_specs=[
            pl.BlockSpec((BLOCK, wide), lambda h, b, *_: (b, first + h)),
            pl.BlockSpec((rows, HD), lambda h, b, *_: (0, first + h)),
            pl.BlockSpec((rows, HD), lambda h, b, *_: (0, first + h)),
            pl.BlockSpec((n, 2, BLOCK, HD), lambda h, b, *_: (0, 0, 0, h)),
        ]
        + ([] if so_far is None else [pl.BlockSpec(memory_space=pl.ANY)]),
        out_specs=pl.BlockSpec((BLOCK, wide), lambda h, b, *_: (b, first + h)),
        scratch_shapes=[
            pltpu.VMEM((chosen // 2 + 2, wide // HD * BLOCK, 2 * BLOCK), F32),
            pltpu.VMEM((wide // HD * BLOCK, BLOCK), F32),
            pltpu.VMEM((wide // HD * BLOCK, BLOCK), F32),
            pltpu.VMEM((wide // HD * BLOCK, BLOCK), F32),
        ],
    )
    return pl.pallas_call(
        functools.partial(soft_kernel, chosen),
        out_shape=jax.ShapeDtypeStruct((rows, features), BF16),
        grid_spec=grid_spec,
        input_output_aliases={} if so_far is None else {6: 0},
        compiler_params=params(),
        cost_estimate=cost(9 * kv_here),
        name="soft_attention",
    )(owners, counts, queries, slab_k, slab_v, arrived, *(() if so_far is None else (so_far,)))


def parts_of(kv_count):
    return [kv_count] if kv_count < 2 else [kv_count - 1, 1]


def local(
    lin_queries,
    lin_keys,
    lin_values,
    log_decay,
    lin_gate,
    norm_gain,
    soft_queries,
    slab_keys,
    slab_values,
    cache_keys,
    cache_values,
    block_lists,
    live_counts,
):
    n = lax.axis_size("ctx")
    me = lax.axis_index("ctx")
    head_devices = lax.axis_size("head")
    heads = log_decay.shape[1]
    chosen = block_lists.shape[1]
    kv_count = cache_keys.shape[1] // HD
    stored = cache_keys.shape[0] // BLOCK
    blocks_here = block_lists.shape[0] // n
    group = 1
    while group < 8 and 2 * group <= n and heads % (2 * group) == 0:
        group *= 2
    per = heads // group

    lists = block_lists.reshape(n, blocks_here, chosen)
    counts = live_counts.reshape(n, blocks_here)
    live = jnp.arange(chosen)[None, None, :] < counts[:, :, None]
    owner = lists // stored
    spots = jnp.max(jnp.where(live & (owner == me), lists % stored, 0), axis=(1, 2))
    my_owners = lax.dynamic_slice_in_dim(owner, me, 1, 0).reshape(blocks_here * chosen)
    my_counts = lax.dynamic_slice_in_dim(counts, me, 1, 0).reshape(blocks_here)
    place = (me % group).reshape(1)

    parts = parts_of(kv_count)
    outgoing = pack(spots, cache_keys, cache_values, 0, [part * HD for part in parts])

    running, *messages = segment_states(lin_keys, lin_values, log_decay, place, group)
    messages = exchange_in_group(messages, group)
    (total,) = walk(messages, place)
    logs = None
    if n // group > 2:
        logs = sum(
            message[per * HD : per * HD + 3 * per, 0].astype(F32).reshape(3, per).sum(0)
            for message in messages
        )
        logs = jnp.repeat(logs, HD)
    before = states_before_group(total, logs, group)
    states = exchange_in_group(walk(messages, place, before), group)

    inside = intra(lin_queries, lin_keys, lin_values, running)
    attn, squares = join(lin_queries, inside, running, states, place)
    arrived = [lax.all_to_all(outgoing[0], "ctx", 0, 0, tiled=True)]
    for block in outgoing[1:]:
        block, attn = lax.optimization_barrier((block, attn))
        arrived.append(lax.all_to_all(block, "ctx", 0, 0, tiled=True))
    summands = [squares]
    reach = 1
    while reach < head_devices:
        if len(summands) > 1:
            summands = [summands[0] + summands[1]]
        summands.append(
            lax.ppermute(summands[0], "head", [(i, i ^ reach) for i in range(head_devices)])
        )
        reach *= 2
    features = head_devices * heads * HD
    lin_out = gated(attn, lin_gate, norm_gain, summands, features)

    soft_out = None
    first = 0
    for part, block in zip(parts, arrived):
        soft_out = soft_part(
            my_owners, my_counts, soft_queries, slab_keys, slab_values, block, first, chosen, soft_out
        )
        first += part
    return (lin_out, soft_out)


def solution(mesh):
    in_specs = (
        P("ctx", "head"),
        P("ctx", "head"),
        P("ctx", "head"),
        P("ctx", "head"),
        P("ctx", "head"),
        P("head"),
        P("ctx", "head"),
        P("ctx", "head"),
        P("ctx", "head"),
        P("ctx", "head"),
        P("ctx", "head"),
        P(),
        P(),
    )
    out_specs = (P("ctx", "head"), P("ctx", "head"))
    return jax.shard_map(local, mesh=mesh, in_specs=in_specs, out_specs=out_specs, check_vma=False)
```

```python
import functools
import math

import jax
import jax.numpy as jnp
from jax import lax
from jax.experimental import pallas as pl
from jax.experimental.pallas import tpu as pltpu
from jax.sharding import PartitionSpec as P

HD = 128
BLOCK = 128
STEP_HEADS = 8
GROUP = 4
VMEM_LIMIT = 56 * 1024 * 1024
F32 = jnp.float32
BF16 = jnp.bfloat16
NT = (((1,), (1,)), ((), ()))
NN = (((1,), (0,)), ((), ()))


def tail_rows(per):
    return -(-3 * per // 16) * 16


def split_logs(logs):
    high = logs.astype(BF16).astype(F32)
    middle = (logs - high).astype(BF16).astype(F32)
    rows = [high, middle, logs - high - middle]
    spare = tail_rows(logs.shape[0]) - 3 * logs.shape[0]
    if spare:
        rows.append(jnp.zeros((spare, HD), F32))
    return jnp.concatenate(rows, axis=0).astype(BF16)


def params(**more):
    return pltpu.CompilerParams(vmem_limit_bytes=VMEM_LIMIT, **more)


def cost(microseconds):
    return pl.CostEstimate(
        flops=0, bytes_accessed=int(microseconds * 3.69e6), transcendentals=0
    )


def silu(u):
    half = u.astype(F32) * 0.5
    return (half + half * jnp.tanh(half)).astype(BF16)


def pack_kernel(first, spots, keys, values, *rest):
    outs, sems = rest[:-1], rest[-1]
    copies = []
    start = first
    for part, out in enumerate(outs):
        width = out.shape[3]
        for dest in range(out.shape[0]):
            rows = pl.ds(pl.multiple_of(spots[dest] * BLOCK, BLOCK), BLOCK)
            for kind, source in enumerate((keys, values)):
                copies.append(
                    pltpu.make_async_copy(
                        source.at[rows, pl.ds(start, width)],
                        out.at[dest, kind],
                        sems.at[part, dest, kind],
                    )
                )
        start += width
    for copy in copies:
        copy.start()
    for copy in copies:
        copy.wait()


def pack(spots, keys, values, first, widths):
    n = spots.shape[0]
    whole = pl.BlockSpec(keys.shape, lambda i, _: (0, 0))
    return pl.pallas_call(
        functools.partial(pack_kernel, first),
        out_shape=[jax.ShapeDtypeStruct((n, 2, BLOCK, width), BF16) for width in widths],
        grid_spec=pltpu.PrefetchScalarGridSpec(
            num_scalar_prefetch=1,
            grid=(1,),
            in_specs=[whole, whole],
            out_specs=[pl.BlockSpec(memory_space=pl.ANY)] * len(widths),
            scratch_shapes=[pltpu.SemaphoreType.DMA((len(widths), n, 2))],
        ),
        compiler_params=params(),
        cost_estimate=cost(4),
        name="pack",
    )(spots, keys, values)


def state_kernel(group, place, keys, values, decay, running_out, *rest):
    outs, running, hold = rest[:group], rest[group], rest[group + 1]
    step = pl.program_id(0)
    rows = keys.shape[0]
    mine = place[0]
    per = running.shape[0] // group

    @pl.when(step == 0)
    def _():
        s = lax.broadcasted_iota(jnp.int32, (rows, rows), 0)
        t = lax.broadcasted_iota(jnp.int32, (rows, rows), 1)
        running[...] = lax.dot_general(
            decay[...],
            (s <= t).astype(F32),
            NN,
            precision=lax.Precision.HIGHEST,
            preferred_element_type=F32,
        )

    here = running[pl.ds(pl.multiple_of(step * STEP_HEADS, STEP_HEADS), STEP_HEADS), :]
    running_out[...] = here
    total = here[:, rows - 1 : rows]
    fade = jnp.exp(total - here)
    logs = jnp.broadcast_to(total, (STEP_HEADS, HD))
    for dest in range(STEP_HEADS // per):
        slot = (step * (STEP_HEADS // per) + dest) ^ mine
        for i in range(per):
            head = dest * per + i
            columns = slice(head * HD, (head + 1) * HD)
            act = silu(keys[:, columns]).T
            state = jnp.dot(
                (act.astype(F32) * fade[head : head + 1, :]).astype(BF16),
                values[:, columns],
                preferred_element_type=F32,
            )
            hold[slot, i * HD : (i + 1) * HD, :] = state.astype(BF16)
        hold[slot, per * HD :, :] = split_logs(logs[dest * per : (dest + 1) * per])

    @pl.when(step == pl.num_programs(0) - 1)
    def _():
        for k, out in enumerate(outs):
            out[...] = hold[k]


def segment_states(keys, values, decay, place, group):
    heads, rows = decay.shape
    per = heads // group
    size = per * HD + tail_rows(per)
    wide = STEP_HEADS * HD
    return pl.pallas_call(
        functools.partial(state_kernel, group),
        out_shape=[jax.ShapeDtypeStruct((heads, rows), F32)]
        + [jax.ShapeDtypeStruct((size, HD), BF16)] * group,
        grid_spec=pltpu.PrefetchScalarGridSpec(
            num_scalar_prefetch=1,
            grid=(heads // STEP_HEADS,),
            in_specs=[
                pl.BlockSpec((rows, wide), lambda i, _: (0, i)),
                pl.BlockSpec((rows, wide), lambda i, _: (0, i)),
                pl.BlockSpec((heads, rows), lambda i, _: (0, 0)),
            ],
            out_specs=[pl.BlockSpec((STEP_HEADS, rows), lambda i, _: (i, 0))]
            + [pl.BlockSpec((size, HD), lambda i, _: (0, 0))] * group,
            scratch_shapes=[pltpu.VMEM((heads, rows), F32), pltpu.VMEM((group, size, HD), BF16)],
        ),
        compiler_params=params(),
        cost_estimate=cost(6),
        name="segment_states",
    )(place, keys, values, decay)


def intra_kernel(queries, keys, values, running, out):
    rows = queries.shape[0]
    column = running[...].T
    t = lax.broadcasted_iota(jnp.int32, (BLOCK, BLOCK), 0)
    s = lax.broadcasted_iota(jnp.int32, (BLOCK, BLOCK), 1)
    causal = s <= t
    for head in range(STEP_HEADS):
        columns = slice(head * HD, (head + 1) * HD)
        act_q = silu(queries[:, columns])
        act_k = silu(keys[:, columns])
        v = values[:, columns]
        for a in range(rows // BLOCK):
            mine = slice(a * BLOCK, (a + 1) * BLOCK)
            seen = (a + 1) * BLOCK
            scores = lax.dot_general(act_q[mine], act_k[:seen], NT, preferred_element_type=F32)
            gaps = column[mine, head : head + 1] - running[head : head + 1, :seen]
            pieces = []
            for b in range(a + 1):
                part = slice(b * BLOCK, (b + 1) * BLOCK)
                gap = jnp.minimum(gaps[:, part], 0.0)
                if b == a:
                    gap = jnp.where(causal, gap, -1e30)
                pieces.append((scores[:, part] * jnp.exp(gap)).astype(BF16))
            weights = pieces[0] if a == 0 else jnp.concatenate(pieces, axis=1)
            out[mine, columns] = jnp.dot(weights, v[:seen], preferred_element_type=F32)


def intra(queries, keys, values, running):
    rows, features = queries.shape
    wide = STEP_HEADS * HD
    block = pl.BlockSpec((rows, wide), lambda i: (0, i))
    return pl.pallas_call(
        intra_kernel,
        out_shape=jax.ShapeDtypeStruct((rows, features), F32),
        grid=(features // wide,),
        in_specs=[block, block, block, pl.BlockSpec((STEP_HEADS, rows), lambda i: (i, 0))],
        out_specs=block,
        compiler_params=params(),
        cost_estimate=cost(10),
        name="intra",
    )(queries, keys, values, running)


def read_logs(message, per):
    tail = message[per * HD :, :].astype(F32)
    return tail[:per] + tail[per : 2 * per] + tail[2 * per : 3 * per]


def total_kernel(group, per, place, *refs):
    arrived, out, hold = refs[:group], refs[group], refs[group + 1]
    for k in range(group):
        hold[place[0] ^ k] = arrived[k][...]
    logs = [read_logs(hold.at[j], per) for j in range(group)]
    fades = [jnp.exp(log) for log in logs]
    for head in range(per):
        rows = slice(head * HD, (head + 1) * HD)
        state = hold[0, rows, :].astype(F32)
        for j in range(1, group):
            state = fades[j][head : head + 1, :] * state + hold[j, rows, :].astype(F32)
        out[rows, :] = state.astype(BF16)
    out[per * HD :, :] = split_logs(functools.reduce(lambda x, y: x + y, logs))


def enter_kernel(group, per, place, *refs):
    arrived, earlier, refs = refs[:group], refs[group : -group - 1], refs[-group - 1 :]
    outs, hold = refs[:-1], refs[-1]
    for k in range(group):
        hold[place[0] ^ k] = arrived[k][...]
    fades = [jnp.exp(read_logs(hold.at[j], per)) for j in range(group)]
    passed = [jnp.exp(read_logs(message, per)) for message in earlier]
    for head in range(per):
        rows = slice(head * HD, (head + 1) * HD)
        state = jnp.zeros((HD, HD), F32)
        for message, fade in zip(earlier, passed):
            state = fade[head : head + 1, :] * state + message[rows, :].astype(F32)
        for j in range(group):
            own = hold[j, rows, :].astype(F32)
            hold[j, rows, :] = state.astype(BF16)
            state = fades[j][head : head + 1, :] * state + own
    for k in range(group):
        outs[k][...] = hold[place[0] ^ k, : per * HD, :]


def walk(kernel, arrived, earlier, place, per):
    group = len(arrived)
    size = arrived[0].shape[0]
    message = pl.BlockSpec((size, HD), lambda i, _: (0, 0))
    state = pl.BlockSpec((per * HD, HD), lambda i, _: (0, 0))
    out_shape, out_specs = jax.ShapeDtypeStruct((size, HD), BF16), message
    if kernel is enter_kernel:
        out_shape = [jax.ShapeDtypeStruct((per * HD, HD), BF16)] * group
        out_specs = [state] * group
    return pl.pallas_call(
        functools.partial(kernel, group, per),
        out_shape=out_shape,
        grid_spec=pltpu.PrefetchScalarGridSpec(
            num_scalar_prefetch=1,
            grid=(1,),
            in_specs=[message] * (group + len(earlier)),
            out_specs=out_specs,
            scratch_shapes=[pltpu.VMEM((group, size, HD), BF16)],
        ),
        compiler_params=params(),
        cost_estimate=cost(2.5),
        name="walk_states",
    )(place, *arrived, *earlier)


def join_kernel(group, place, queries, inside, running, *refs):
    states, (out, squares), (hold, total) = refs[:group], refs[group : group + 2], refs[group + 2 :]
    step = pl.program_id(0)
    mine = place[0]
    per = hold.shape[1] // HD

    @pl.when(step == 0)
    def _():
        for k in range(group):
            hold[mine ^ k] = states[k][...]
        total[...] = jnp.zeros_like(total)

    grow = jnp.exp(running[...].T)
    summed = jnp.zeros(total.shape, F32)
    for head in range(STEP_HEADS):
        columns = slice(head * HD, (head + 1) * HD)
        owner = step * (STEP_HEADS // per) + head // per
        part = (head % per) * HD
        passed = jnp.dot(
            silu(queries[:, columns]), hold[owner, part : part + HD, :], preferred_element_type=F32
        )
        attn = inside[:, columns] + grow[:, head : head + 1] * passed
        out[:, columns] = attn
        summed += attn * attn
    total[...] += summed

    @pl.when(step == pl.num_programs(0) - 1)
    def _():
        squares[...] = lax.dot_general(
            jnp.ones((8, HD), F32),
            total[...],
            NT,
            precision=lax.Precision.HIGHEST,
            preferred_element_type=F32,
        )


def join(queries, inside, running, states, place):
    rows, features = queries.shape
    wide = STEP_HEADS * HD
    block = pl.BlockSpec((rows, wide), lambda i, _: (0, i))
    group = len(states)
    return pl.pallas_call(
        functools.partial(join_kernel, group),
        out_shape=[
            jax.ShapeDtypeStruct((rows, features), F32),
            jax.ShapeDtypeStruct((8, rows), F32),
        ],
        grid_spec=pltpu.PrefetchScalarGridSpec(
            num_scalar_prefetch=1,
            grid=(features // wide,),
            in_specs=[block, block, pl.BlockSpec((STEP_HEADS, rows), lambda i, _: (i, 0))]
            + [pl.BlockSpec(state.shape, lambda i, _: (0, 0)) for state in states],
            out_specs=[block, pl.BlockSpec((8, rows), lambda i, _: (0, 0))],
            scratch_shapes=[
                pltpu.VMEM((group,) + states[0].shape, BF16),
                pltpu.VMEM((rows, HD), F32),
            ],
        ),
        compiler_params=params(),
        cost_estimate=cost(7),
        name="join_states",
    )(place, queries, inside, running, *states)


def gate_kernel(features, attn, gate, gain, *refs):
    out = refs[-1]
    squares = refs[0][...]
    for more in refs[1:-1]:
        squares = squares + more[...]
    scaling = lax.rsqrt(squares / features + 1e-06).T[:, :1]
    half = gate[...].astype(F32) * 0.5
    opened = 0.5 + 0.5 * jnp.tanh(half)
    out[...] = (attn[...] * scaling * gain[...] * opened).astype(BF16)


def gated(attn, gate, gain, squares, features):
    rows, here = attn.shape
    wide = STEP_HEADS * HD
    block = pl.BlockSpec((rows, wide), lambda i: (0, i))
    return pl.pallas_call(
        functools.partial(gate_kernel, features),
        out_shape=jax.ShapeDtypeStruct((rows, here), BF16),
        grid=(here // wide,),
        in_specs=[block, block, pl.BlockSpec((1, wide), lambda i: (0, i))]
        + [pl.BlockSpec((8, rows), lambda i: (0, 0))] * len(squares),
        out_specs=block,
        compiler_params=params(),
        cost_estimate=cost(6),
        name="gated_norm",
    )(attn, gate, gain.reshape(1, here), *squares)


def exchange_in_group(messages, group):
    n = lax.axis_size("ctx")
    return [messages[0]] + [
        lax.ppermute(messages[k], "ctx", [(i, i ^ k) for i in range(n)]) for k in range(1, group)
    ]


def groups_before(total, group):
    n = lax.axis_size("ctx")
    return [
        lax.ppermute(total, "ctx", [(i, i + by) for i in range(n - by)])
        for by in range(n - group, 0, -group)
    ]


def soft_kernel(chosen, owners, counts, queries, slab_k, slab_v, arrived, *refs):
    out, top, weight_sum, mixed = refs[-4:]
    b = pl.program_id(1)
    count = counts[b]
    heads = queries.shape[1] // HD
    rows = min(4, heads) * BLOCK
    chunks = heads * BLOCK // rows
    scale = math.log2(math.e) / math.sqrt(HD)

    def spans():
        return [(r, slice(r * rows, (r + 1) * rows)) for r in range(chunks)]

    def queries_of(r):
        per = rows // BLOCK
        parts = [queries[:, (per * r + i) * HD : (per * r + i + 1) * HD] for i in range(per)]
        return jnp.concatenate(parts, axis=0)

    def fetch(kind, first, number):
        parts = [arrived[owners[b * chosen + first + i], kind] for i in range(number)]
        return parts[0] if number == 1 else jnp.concatenate(parts, axis=0)

    t = lax.broadcasted_iota(jnp.int32, (rows, slab_k.shape[0]), 0) % BLOCK
    s_at = lax.broadcasted_iota(jnp.int32, (rows, slab_k.shape[0]), 1)
    causal = s_at <= t + b * BLOCK

    def weigh(scores, highest):
        number = scores.shape[1] // BLOCK
        parts = [
            jnp.exp2(scores[:, i * BLOCK : (i + 1) * BLOCK] * scale - highest)
            for i in range(number)
        ]
        summed = functools.reduce(lambda x, y: x + y, parts)
        parts = [part.astype(BF16) for part in parts]
        return summed, parts[0] if number == 1 else jnp.concatenate(parts, axis=1)

    def cached(first, number):
        k, v = fetch(0, first, number), fetch(1, first, number)
        for r, at in spans():
            scores = lax.dot_general(queries_of(r), k, NT, preferred_element_type=F32)
            summed, w = weigh(scores, top[at, :])
            weight_sum[at, :] += summed
            mixed[at, :] += jnp.dot(w, v, preferred_element_type=F32)

    def raise_top(j):
        k = fetch(0, j, 1)
        for r, at in spans():
            scores = lax.dot_general(queries_of(r), k, NT, preferred_element_type=F32)
            here = jnp.max(scores, axis=1, keepdims=True) * scale
            top[at, :] = jnp.maximum(top[at, :], here)

    def attempt(again):
        for r, at in spans():
            scores = lax.dot_general(queries_of(r), slab_k[...], NT, preferred_element_type=F32)
            scores = jnp.where(causal, scores, -1e30)
            highest = jnp.max(scores, axis=1, keepdims=True) * scale
            top[at, :] = jnp.maximum(top[at, :], highest)
            summed, w = weigh(scores, top[at, :])
            weight_sum[at, :] = summed
            mixed[at, :] = jnp.dot(w, slab_v[...], preferred_element_type=F32)

        def eight(p, carry):
            cached(8 * p, 8)
            return carry

        lax.fori_loop(0, count // 8, eight, 0)
        for number in (4, 2, 1):

            @pl.when((count // number) % 2 == 1)
            def _(number=number):
                cached((count // (2 * number)) * (2 * number), number)

        fine = jnp.max(weight_sum[...]) < 1e25

        @pl.when(jnp.logical_not(fine))
        def _():
            def turn(j, carry):
                raise_top(j)
                return carry

            lax.fori_loop(0, count, turn, 0)

        return jnp.logical_not(fine)

    top[...] = jnp.full(top.shape, -1e30, F32)
    lax.while_loop(lambda again: again, attempt, jnp.bool_(True))
    for head in range(heads):
        at = slice(head * BLOCK, (head + 1) * BLOCK)
        total = jnp.sum(weight_sum[at, :], axis=1, keepdims=True)
        out[:, head * HD : (head + 1) * HD] = (mixed[at, :] / total).astype(BF16)


def soft_part(owners, counts, queries, slab_k, slab_v, arrived, first, chosen, so_far):
    rows, features = queries.shape
    kv_here = arrived.shape[3] // HD
    n = arrived.shape[0]
    wide = features // (slab_k.shape[1] // HD)
    blocks = rows // BLOCK
    grid_spec = pltpu.PrefetchScalarGridSpec(
        num_scalar_prefetch=2,
        grid=(kv_here, blocks),
        in_specs=[
            pl.BlockSpec((BLOCK, wide), lambda h, b, *_: (b, first + h)),
            pl.BlockSpec((rows, HD), lambda h, b, *_: (0, first + h)),
            pl.BlockSpec((rows, HD), lambda h, b, *_: (0, first + h)),
            pl.BlockSpec((n, 2, BLOCK, HD), lambda h, b, *_: (0, 0, 0, h)),
        ]
        + ([] if so_far is None else [pl.BlockSpec(memory_space=pl.ANY)]),
        out_specs=pl.BlockSpec((BLOCK, wide), lambda h, b, *_: (b, first + h)),
        scratch_shapes=[
            pltpu.VMEM((wide // HD * BLOCK, BLOCK), F32),
            pltpu.VMEM((wide // HD * BLOCK, BLOCK), F32),
            pltpu.VMEM((wide // HD * BLOCK, BLOCK), F32),
        ],
    )
    return pl.pallas_call(
        functools.partial(soft_kernel, chosen),
        out_shape=jax.ShapeDtypeStruct((rows, features), BF16),
        grid_spec=grid_spec,
        input_output_aliases={} if so_far is None else {6: 0},
        compiler_params=params(),
        cost_estimate=cost(8 * kv_here),
        name="soft_attention",
    )(owners, counts, queries, slab_k, slab_v, arrived, *(() if so_far is None else (so_far,)))


def parts_of(kv_count):
    return [kv_count - kv_count // 2, kv_count // 2] if kv_count > 1 else [1]


def local(
    lin_queries,
    lin_keys,
    lin_values,
    log_decay,
    lin_gate,
    norm_gain,
    soft_queries,
    slab_keys,
    slab_values,
    cache_keys,
    cache_values,
    block_lists,
    live_counts,
):
    n = lax.axis_size("ctx")
    me = lax.axis_index("ctx")
    head_devices = lax.axis_size("head")
    heads = log_decay.shape[1]
    chosen = block_lists.shape[1]
    kv_count = cache_keys.shape[1] // HD
    stored = cache_keys.shape[0] // BLOCK
    blocks_here = block_lists.shape[0] // n
    group = 1
    while group < GROUP and 2 * group <= n and heads % (2 * group) == 0:
        group *= 2
    per = heads // group

    lists = block_lists.reshape(n, blocks_here, chosen)
    counts = live_counts.reshape(n, blocks_here)
    live = jnp.arange(chosen)[None, None, :] < counts[:, :, None]
    owner = lists // stored
    spots = jnp.max(jnp.where(live & (owner == me), lists % stored, 0), axis=(1, 2))
    my_owners = lax.dynamic_slice_in_dim(owner, me, 1, 0).reshape(blocks_here * chosen)
    my_counts = lax.dynamic_slice_in_dim(counts, me, 1, 0).reshape(blocks_here)
    place = (me % group).reshape(1)

    tied = lax.optimization_barrier
    parts = parts_of(kv_count)
    widths = [part * HD for part in parts]
    outgoing = list(pack(spots, cache_keys, cache_values, 0, widths[:1]))
    arrived = [lax.all_to_all(outgoing[0], "ctx", 0, 0, tiled=True)]

    running, *messages = segment_states(lin_keys, lin_values, log_decay.T, place, group)
    messages = exchange_in_group(messages, group)
    inside = intra(lin_queries, lin_keys, lin_values, running)
    if len(parts) > 1:
        outgoing += pack(spots, cache_keys, cache_values, widths[0], widths[1:])
        inside, outgoing[1], messages[1] = tied((inside, outgoing[1], messages[1]))
    total = walk(total_kernel, messages, (), place, per)
    earlier = groups_before(total, group)
    if len(parts) > 1:
        block, arrived[0], *earlier = tied((outgoing[1], arrived[0], *earlier))
        arrived.append(lax.all_to_all(block, "ctx", 0, 0, tiled=True))
    states = exchange_in_group(walk(enter_kernel, messages, earlier, place, per), group)

    def attend(i, so_far):
        return soft_part(
            my_owners,
            my_counts,
            soft_queries,
            slab_keys,
            slab_values,
            arrived[i],
            sum(parts[:i]),
            chosen,
            so_far,
        )

    soft_out = None
    if len(parts) > 1:
        soft_out = attend(0, None)
        soft_out, running = tied((soft_out, running))
    attn, squares = join(lin_queries, inside, running, states, place)
    summands = [squares]
    reach = 1
    while reach < head_devices:
        if len(summands) > 1:
            summands = [summands[0] + summands[1]]
        summands.append(
            lax.ppermute(summands[0], "head", [(i, i ^ reach) for i in range(head_devices)])
        )
        reach *= 2
    features = head_devices * heads * HD
    lin_out = gated(attn, lin_gate, norm_gain, summands, features)
    if len(parts) > 1:
        lin_out, my_owners = tied((lin_out, my_owners))
    return (lin_out, attend(len(parts) - 1, soft_out))


def solution(mesh):
    in_specs = (
        P("ctx", "head"),
        P("ctx", "head"),
        P("ctx", "head"),
        P("ctx", "head"),
        P("ctx", "head"),
        P("head"),
        P("ctx", "head"),
        P("ctx", "head"),
        P("ctx", "head"),
        P("ctx", "head"),
        P("ctx", "head"),
        P(),
        P(),
    )
    out_specs = (P("ctx", "head"), P("ctx", "head"))
    return jax.shard_map(local, mesh=mesh, in_specs=in_specs, out_specs=out_specs, check_vma=False)
```

```python
import functools
import math

import jax
import jax.numpy as jnp
from jax import lax
from jax.experimental import pallas as pl
from jax.experimental.pallas import tpu as pltpu
from jax.sharding import PartitionSpec as P

HD = 128
BLOCK = 128
STEP_HEADS = 8
GROUP = 4
VMEM_LIMIT = 28 * 1024 * 1024
IN_VMEM = pl.BlockSpec(memory_space=pltpu.VMEM)
F32 = jnp.float32
BF16 = jnp.bfloat16
NT = (((1,), (1,)), ((), ()))
NN = (((1,), (0,)), ((), ()))


def tail_rows(per):
    return -(-3 * per // 16) * 16


def split_logs(logs):
    high = logs.astype(BF16).astype(F32)
    middle = (logs - high).astype(BF16).astype(F32)
    rows = [high, middle, logs - high - middle]
    spare = tail_rows(logs.shape[0]) - 3 * logs.shape[0]
    if spare:
        rows.append(jnp.zeros((spare, HD), F32))
    return jnp.concatenate(rows, axis=0).astype(BF16)


def params(limit=VMEM_LIMIT):
    return pltpu.CompilerParams(vmem_limit_bytes=limit)


def cost(microseconds):
    return pl.CostEstimate(
        flops=0, bytes_accessed=int(microseconds * 3.69e6), transcendentals=0
    )


def silu(u):
    half = u.astype(F32) * 0.5
    return (half + half * jnp.tanh(half)).astype(BF16)


def pack_kernel(first, spots, keys, values, *rest):
    outs, sems = rest[:-1], rest[-1]
    copies = []
    start = first
    for part, out in enumerate(outs):
        width = out.shape[3]
        for dest in range(out.shape[0]):
            rows = pl.ds(pl.multiple_of(spots[dest] * BLOCK, BLOCK), BLOCK)
            for kind, source in enumerate((keys, values)):
                copies.append(
                    pltpu.make_async_copy(
                        source.at[rows, pl.ds(start, width)],
                        out.at[dest, kind],
                        sems.at[part, dest, kind],
                    )
                )
        start += width
    for copy in copies:
        copy.start()
    for copy in copies:
        copy.wait()


def pack(spots, keys, values, first, widths):
    n = spots.shape[0]
    span, column = keys.shape[1], 0
    if first % sum(widths) == 0:
        span, column, first = sum(widths), first // sum(widths), 0
    whole = pl.BlockSpec((keys.shape[0], span), lambda i, _: (0, column))
    return pl.pallas_call(
        functools.partial(pack_kernel, first),
        out_shape=[jax.ShapeDtypeStruct((n, 2, BLOCK, width), BF16) for width in widths],
        grid_spec=pltpu.PrefetchScalarGridSpec(
            num_scalar_prefetch=1,
            grid=(1,),
            in_specs=[whole, whole],
            out_specs=[pl.BlockSpec(memory_space=pl.ANY)] * len(widths),
            scratch_shapes=[pltpu.SemaphoreType.DMA((len(widths), n, 2))],
        ),
        compiler_params=params(58 * 1024 * 1024),
        cost_estimate=cost(4),
        name="pack",
    )(spots, keys, values)


def state_kernel(group, place, keys, values, decay, running_out, *rest):
    outs, running, hold = rest[:group], rest[group], rest[group + 1]
    step = pl.program_id(0)
    rows = keys.shape[0]
    mine = place[0]
    per = running.shape[0] // group

    @pl.when(step == 0)
    def _():
        s = lax.broadcasted_iota(jnp.int32, (rows, rows), 0)
        t = lax.broadcasted_iota(jnp.int32, (rows, rows), 1)
        running[...] = lax.dot_general(
            decay[...],
            (s <= t).astype(F32),
            NN,
            precision=lax.Precision.HIGHEST,
            preferred_element_type=F32,
        )

    here = running[pl.ds(pl.multiple_of(step * STEP_HEADS, STEP_HEADS), STEP_HEADS), :]
    running_out[...] = here
    total = here[:, rows - 1 : rows]
    fade = jnp.exp(total - here)
    logs = jnp.broadcast_to(total, (STEP_HEADS, HD))
    for dest in range(STEP_HEADS // per):
        slot = (step * (STEP_HEADS // per) + dest) ^ mine
        for i in range(per):
            head = dest * per + i
            columns = slice(head * HD, (head + 1) * HD)
            act = silu(keys[:, columns]).T
            state = jnp.dot(
                (act.astype(F32) * fade[head : head + 1, :]).astype(BF16),
                values[:, columns],
                preferred_element_type=F32,
            )
            hold[slot, i * HD : (i + 1) * HD, :] = state.astype(BF16)
        hold[slot, per * HD :, :] = split_logs(logs[dest * per : (dest + 1) * per])

    @pl.when(step == pl.num_programs(0) - 1)
    def _():
        for k, out in enumerate(outs):
            out[...] = hold[k]


def segment_states(keys, values, decay, place, group):
    heads, rows = decay.shape
    per = heads // group
    size = per * HD + tail_rows(per)
    wide = STEP_HEADS * HD
    return pl.pallas_call(
        functools.partial(state_kernel, group),
        out_shape=[jax.ShapeDtypeStruct((heads, rows), F32)]
        + [jax.ShapeDtypeStruct((size, HD), BF16)] * group,
        grid_spec=pltpu.PrefetchScalarGridSpec(
            num_scalar_prefetch=1,
            grid=(heads // STEP_HEADS,),
            in_specs=[
                pl.BlockSpec((rows, wide), lambda i, _: (0, i)),
                pl.BlockSpec((rows, wide), lambda i, _: (0, i)),
                pl.BlockSpec((heads, rows), lambda i, _: (0, 0)),
            ],
            out_specs=[pl.BlockSpec((STEP_HEADS, rows), lambda i, _: (i, 0))]
            + [pl.BlockSpec((size, HD), lambda i, _: (0, 0))] * group,
            scratch_shapes=[pltpu.VMEM((heads, rows), F32), pltpu.VMEM((group, size, HD), BF16)],
        ),
        compiler_params=params(),
        cost_estimate=cost(6),
        name="segment_states",
    )(place, keys, values, decay)


def intra_kernel(queries, keys, values, running, out):
    rows = queries.shape[0]
    column = running[...].T
    t = lax.broadcasted_iota(jnp.int32, (BLOCK, BLOCK), 0)
    s = lax.broadcasted_iota(jnp.int32, (BLOCK, BLOCK), 1)
    causal = s <= t
    for head in range(STEP_HEADS):
        columns = slice(head * HD, (head + 1) * HD)
        act_q = silu(queries[:, columns])
        act_k = silu(keys[:, columns])
        v = values[:, columns]
        for a in range(rows // BLOCK):
            mine = slice(a * BLOCK, (a + 1) * BLOCK)
            seen = (a + 1) * BLOCK
            scores = lax.dot_general(act_q[mine], act_k[:seen], NT, preferred_element_type=F32)
            gaps = column[mine, head : head + 1] - running[head : head + 1, :seen]
            pieces = []
            for b in range(a + 1):
                part = slice(b * BLOCK, (b + 1) * BLOCK)
                gap = jnp.minimum(gaps[:, part], 0.0)
                if b == a:
                    gap = jnp.where(causal, gap, -1e30)
                pieces.append((scores[:, part] * jnp.exp(gap)).astype(BF16))
            weights = pieces[0] if a == 0 else jnp.concatenate(pieces, axis=1)
            out[mine, columns] = jnp.dot(weights, v[:seen], preferred_element_type=F32)


def intra(queries, keys, values, running):
    rows, features = queries.shape
    wide = STEP_HEADS * HD
    block = pl.BlockSpec((rows, wide), lambda i: (0, i))
    return pl.pallas_call(
        intra_kernel,
        out_shape=jax.ShapeDtypeStruct((rows, features), F32),
        grid=(features // wide,),
        in_specs=[block, block, block, pl.BlockSpec((STEP_HEADS, rows), lambda i: (i, 0))],
        out_specs=block,
        compiler_params=params(),
        cost_estimate=cost(10),
        name="intra",
    )(queries, keys, values, running)


def read_logs(message, per):
    tail = message[per * HD :, :].astype(F32)
    return tail[:per] + tail[per : 2 * per] + tail[2 * per : 3 * per]


def total_kernel(group, per, place, *refs):
    arrived, out, hold = refs[:group], refs[group], refs[group + 1]
    for k in range(group):
        hold[place[0] ^ k] = arrived[k][...]
    logs = [read_logs(hold.at[j], per) for j in range(group)]
    fades = [jnp.exp(log) for log in logs]
    for head in range(per):
        rows = slice(head * HD, (head + 1) * HD)
        state = hold[0, rows, :].astype(F32)
        for j in range(1, group):
            state = fades[j][head : head + 1, :] * state + hold[j, rows, :].astype(F32)
        out[rows, :] = state.astype(BF16)
    out[per * HD :, :] = split_logs(functools.reduce(lambda x, y: x + y, logs))


def merge_kernel(group, per, bit, place, mine, partner, out):
    later = (place[1] >> bit) % 2 == 1
    logs = [read_logs(mine, per), read_logs(partner, per)]
    fade = jnp.exp(jnp.where(later, logs[0], logs[1]))
    for head in range(per):
        rows = slice(head * HD, (head + 1) * HD)
        own, other = mine[rows, :].astype(F32), partner[rows, :].astype(F32)
        first, second = jnp.where(later, other, own), jnp.where(later, own, other)
        out[rows, :] = (fade[head : head + 1, :] * first + second).astype(BF16)
    out[per * HD :, :] = split_logs(logs[0] + logs[1])


def enter_kernel(group, per, place, *refs):
    arrived, partners, refs = refs[:group], refs[group : -group - 1], refs[-group - 1 :]
    outs, hold = refs[:-1], refs[-1]
    for k in range(group):
        hold[place[0] ^ k] = arrived[k][...]
    fades = [jnp.exp(read_logs(hold.at[j], per)) for j in range(group)]
    before = [(place[1] >> bit) % 2 == 1 for bit in range(len(partners))]
    passed, log = [], jnp.zeros((per, HD), F32)
    for bit, partner in enumerate(partners):
        passed.append(jnp.exp(log))
        log = log + jnp.where(before[bit], read_logs(partner, per), 0.0)
    for head in range(per):
        rows = slice(head * HD, (head + 1) * HD)
        state = jnp.zeros((HD, HD), F32)
        for bit, partner in enumerate(partners):
            more = passed[bit][head : head + 1, :] * partner[rows, :].astype(F32)
            state = state + jnp.where(before[bit], more, 0.0)
        for j in range(group):
            own = hold[j, rows, :].astype(F32)
            hold[j, rows, :] = state.astype(BF16)
            state = fades[j][head : head + 1, :] * state + own
    for k in range(group):
        outs[k][...] = hold[place[0] ^ k, : per * HD, :]


def walk(kernel, arrived, partners, place, per):
    group = len(arrived)
    size = arrived[0].shape[0]
    message = pl.BlockSpec((size, HD), lambda i, _: (0, 0))
    state = pl.BlockSpec((per * HD, HD), lambda i, _: (0, 0))
    out_shape, out_specs = jax.ShapeDtypeStruct((size, HD), BF16), message
    if kernel is enter_kernel:
        out_shape = [jax.ShapeDtypeStruct((per * HD, HD), BF16)] * group
        out_specs = [state] * group
    return pl.pallas_call(
        functools.partial(kernel, group, per),
        out_shape=out_shape,
        grid_spec=pltpu.PrefetchScalarGridSpec(
            num_scalar_prefetch=1,
            grid=(1,),
            in_specs=[IN_VMEM] * (group + len(partners)),
            out_specs=out_specs,
            scratch_shapes=[pltpu.VMEM((group, size, HD), BF16)],
        ),
        compiler_params=params(),
        cost_estimate=cost(2.5),
        name="walk_states",
    )(place, *arrived, *partners)


def join_kernel(group, place, queries, inside, running, *refs):
    states, (out, squares), (hold, total) = refs[:group], refs[group : group + 2], refs[group + 2 :]
    step = pl.program_id(0)
    mine = place[0]
    per = hold.shape[1] // HD

    @pl.when(step == 0)
    def _():
        for k in range(group):
            hold[mine ^ k] = states[k][...]
        total[...] = jnp.zeros_like(total)

    grow = jnp.exp(running[...].T)
    summed = jnp.zeros(total.shape, F32)
    for head in range(STEP_HEADS):
        columns = slice(head * HD, (head + 1) * HD)
        owner = step * (STEP_HEADS // per) + head // per
        part = (head % per) * HD
        passed = jnp.dot(
            silu(queries[:, columns]), hold[owner, part : part + HD, :], preferred_element_type=F32
        )
        attn = inside[:, columns] + grow[:, head : head + 1] * passed
        out[:, columns] = attn
        summed += attn * attn
    total[...] += summed

    @pl.when(step == pl.num_programs(0) - 1)
    def _():
        squares[...] = lax.dot_general(
            jnp.ones((8, HD), F32),
            total[...],
            NT,
            precision=lax.Precision.HIGHEST,
            preferred_element_type=F32,
        )


def join(queries, inside, running, states, place):
    rows, features = queries.shape
    wide = STEP_HEADS * HD
    block = pl.BlockSpec((rows, wide), lambda i, _: (0, i))
    group = len(states)
    return pl.pallas_call(
        functools.partial(join_kernel, group),
        out_shape=[
            jax.ShapeDtypeStruct((rows, features), F32),
            jax.ShapeDtypeStruct((8, rows), F32),
        ],
        grid_spec=pltpu.PrefetchScalarGridSpec(
            num_scalar_prefetch=1,
            grid=(features // wide,),
            in_specs=[block, block, pl.BlockSpec((STEP_HEADS, rows), lambda i, _: (i, 0))]
            + [IN_VMEM] * group,
            out_specs=[block, pl.BlockSpec((8, rows), lambda i, _: (0, 0))],
            scratch_shapes=[
                pltpu.VMEM((group,) + states[0].shape, BF16),
                pltpu.VMEM((rows, HD), F32),
            ],
        ),
        compiler_params=params(),
        cost_estimate=cost(7),
        name="join_states",
    )(place, queries, inside, running, *states)


def gate_kernel(features, attn, gate, gain, *refs):
    out = refs[-1]
    squares = refs[0][...]
    for more in refs[1:-1]:
        squares = squares + more[...]
    scaling = lax.rsqrt(squares / features + 1e-06).T[:, :1]
    half = gate[...].astype(F32) * 0.5
    opened = 0.5 + 0.5 * jnp.tanh(half)
    out[...] = (attn[...] * scaling * gain[...] * opened).astype(BF16)


def gated(attn, gate, gain, squares, features):
    rows, here = attn.shape
    wide = STEP_HEADS * HD
    block = pl.BlockSpec((rows, wide), lambda i: (0, i))
    return pl.pallas_call(
        functools.partial(gate_kernel, features),
        out_shape=jax.ShapeDtypeStruct((rows, here), BF16),
        grid=(here // wide,),
        in_specs=[block, block, pl.BlockSpec((1, wide), lambda i: (0, i))]
        + [IN_VMEM] * len(squares),
        out_specs=block,
        compiler_params=params(),
        cost_estimate=cost(6),
        name="gated_norm",
    )(attn, gate, gain.reshape(1, here), *squares)


def exchange_in_group(messages, group):
    n = lax.axis_size("ctx")
    return [messages[0]] + [
        lax.ppermute(messages[k], "ctx", [(i, i ^ k) for i in range(n)]) for k in range(1, group)
    ]


def merge(total, partner, place, per, group, bit):
    message = pl.BlockSpec(total.shape, lambda i, _: (0, 0))
    return pl.pallas_call(
        functools.partial(merge_kernel, group, per, bit),
        out_shape=jax.ShapeDtypeStruct(total.shape, BF16),
        grid_spec=pltpu.PrefetchScalarGridSpec(
            num_scalar_prefetch=1,
            grid=(1,),
            in_specs=[IN_VMEM, IN_VMEM],
            out_specs=message,
        ),
        compiler_params=params(),
        cost_estimate=cost(2),
        name="merge_states",
    )(place, total, partner)


def from_partners(total, place, per, group):
    n = lax.axis_size("ctx")
    partners = []
    reach = group
    while reach < n:
        if partners:
            total = merge(total, partners[-1], place, per, group, len(partners) - 1)
        partners.append(lax.ppermute(total, "ctx", [(i, i ^ reach) for i in range(n)]))
        reach *= 2
    return partners, total


def soft_kernel(chosen, skip, owners, counts, queries, slab_k, slab_v, arrived, *refs):
    out, top, weight_sum, mixed = refs[-4:]
    b = pl.program_id(1)
    count = counts[b]
    columns = pl.ds(pl.multiple_of((skip + pl.program_id(0)) * HD, HD), HD)
    heads = queries.shape[1] // HD
    rows = min(4, heads) * BLOCK
    chunks = heads * BLOCK // rows
    scale = math.log2(math.e) / math.sqrt(HD)

    def spans():
        return [(r, slice(r * rows, (r + 1) * rows)) for r in range(chunks)]

    def queries_of(r):
        per = rows // BLOCK
        parts = [queries[:, (per * r + i) * HD : (per * r + i + 1) * HD] for i in range(per)]
        return jnp.concatenate(parts, axis=0)

    def fetch(kind, first, number):
        parts = [
            arrived[owners[b * chosen + first + i], kind, :, columns] for i in range(number)
        ]
        return parts[0] if number == 1 else jnp.concatenate(parts, axis=0)

    t = lax.broadcasted_iota(jnp.int32, (rows, slab_k.shape[0]), 0) % BLOCK
    s_at = lax.broadcasted_iota(jnp.int32, (rows, slab_k.shape[0]), 1)
    causal = s_at <= t + b * BLOCK

    def weigh(scores, highest):
        number = scores.shape[1] // BLOCK
        parts = [
            jnp.exp2(scores[:, i * BLOCK : (i + 1) * BLOCK] * scale - highest)
            for i in range(number)
        ]
        summed = functools.reduce(lambda x, y: x + y, parts)
        parts = [part.astype(BF16) for part in parts]
        return summed, parts[0] if number == 1 else jnp.concatenate(parts, axis=1)

    def cached(first, number):
        k, v = fetch(0, first, number), fetch(1, first, number)
        for r, at in spans():
            scores = lax.dot_general(queries_of(r), k, NT, preferred_element_type=F32)
            summed, w = weigh(scores, top[at, :])
            weight_sum[at, :] += summed
            mixed[at, :] += jnp.dot(w, v, preferred_element_type=F32)

    def raise_top(j):
        k = fetch(0, j, 1)
        for r, at in spans():
            scores = lax.dot_general(queries_of(r), k, NT, preferred_element_type=F32)
            here = jnp.max(scores, axis=1, keepdims=True) * scale
            top[at, :] = jnp.maximum(top[at, :], here)

    def attempt(again):
        for r, at in spans():
            scores = lax.dot_general(queries_of(r), slab_k[...], NT, preferred_element_type=F32)
            scores = jnp.where(causal, scores, -1e30)
            highest = jnp.max(scores, axis=1, keepdims=True) * scale
            top[at, :] = jnp.maximum(top[at, :], highest)
            summed, w = weigh(scores, top[at, :])
            weight_sum[at, :] = summed
            mixed[at, :] = jnp.dot(w, slab_v[...], preferred_element_type=F32)

        def eight(p, carry):
            cached(8 * p, 8)
            return carry

        lax.fori_loop(0, count // 8, eight, 0)
        for number in (4, 2, 1):

            @pl.when((count // number) % 2 == 1)
            def _(number=number):
                cached((count // (2 * number)) * (2 * number), number)

        fine = jnp.max(weight_sum[...]) < 1e25

        @pl.when(jnp.logical_not(fine))
        def _():
            def turn(j, carry):
                raise_top(j)
                return carry

            lax.fori_loop(0, count, turn, 0)

        return jnp.logical_not(fine)

    top[...] = jnp.full(top.shape, -1e30, F32)
    lax.while_loop(lambda again: again, attempt, jnp.bool_(True))
    for head in range(heads):
        at = slice(head * BLOCK, (head + 1) * BLOCK)
        total = jnp.sum(weight_sum[at, :], axis=1, keepdims=True)
        out[:, head * HD : (head + 1) * HD] = (mixed[at, :] / total).astype(BF16)


def soft_part(owners, counts, queries, slab_k, slab_v, arrived, skip, kv_here, first, chosen, so_far):
    rows, features = queries.shape
    wide = features // (slab_k.shape[1] // HD)
    blocks = rows // BLOCK
    grid_spec = pltpu.PrefetchScalarGridSpec(
        num_scalar_prefetch=2,
        grid=(kv_here, blocks),
        in_specs=[
            pl.BlockSpec((BLOCK, wide), lambda h, b, *_: (b, first + h)),
            pl.BlockSpec((rows, HD), lambda h, b, *_: (0, first + h)),
            pl.BlockSpec((rows, HD), lambda h, b, *_: (0, first + h)),
            IN_VMEM,
        ]
        + ([] if so_far is None else [pl.BlockSpec(memory_space=pl.ANY)]),
        out_specs=pl.BlockSpec((BLOCK, wide), lambda h, b, *_: (b, first + h)),
        scratch_shapes=[
            pltpu.VMEM((wide // HD * BLOCK, BLOCK), F32),
            pltpu.VMEM((wide // HD * BLOCK, BLOCK), F32),
            pltpu.VMEM((wide // HD * BLOCK, BLOCK), F32),
        ],
    )
    return pl.pallas_call(
        functools.partial(soft_kernel, chosen, skip),
        out_shape=jax.ShapeDtypeStruct((rows, features), BF16),
        grid_spec=grid_spec,
        input_output_aliases={} if so_far is None else {6: 0},
        compiler_params=params(),
        cost_estimate=cost(8 * kv_here),
        name="soft_attention",
    )(owners, counts, queries, slab_k, slab_v, arrived, *(() if so_far is None else (so_far,)))


def parts_of(kv_count):
    return [kv_count - kv_count // 2, kv_count // 2] if kv_count > 1 else [1]


def local(
    lin_queries,
    lin_keys,
    lin_values,
    log_decay,
    lin_gate,
    norm_gain,
    soft_queries,
    slab_keys,
    slab_values,
    cache_keys,
    cache_values,
    block_lists,
    live_counts,
):
    n = lax.axis_size("ctx")
    me = lax.axis_index("ctx")
    head_devices = lax.axis_size("head")
    heads = log_decay.shape[1]
    chosen = block_lists.shape[1]
    kv_count = cache_keys.shape[1] // HD
    stored = cache_keys.shape[0] // BLOCK
    blocks_here = block_lists.shape[0] // n
    group = 1
    while group < GROUP and 2 * group <= n and heads % (2 * group) == 0:
        group *= 2
    per = heads // group

    lists = block_lists.reshape(n, blocks_here, chosen)
    counts = live_counts.reshape(n, blocks_here)
    live = jnp.arange(chosen)[None, None, :] < counts[:, :, None]
    owner = lists // stored
    spots = jnp.max(jnp.where(live & (owner == me), lists % stored, 0), axis=(1, 2))
    my_owners = lax.dynamic_slice_in_dim(owner, me, 1, 0).reshape(blocks_here * chosen)
    my_counts = lax.dynamic_slice_in_dim(counts, me, 1, 0).reshape(blocks_here)
    place = (me % group).reshape(1)
    places = jnp.stack([me % group, me // group])

    tied = lax.optimization_barrier
    parts = parts_of(kv_count)
    widths = [part * HD for part in parts]
    outgoing = list(pack(spots, cache_keys, cache_values, 0, widths[:1]))
    arrived = [lax.all_to_all(outgoing[0], "ctx", 0, 0, tiled=True)]

    running, *messages = segment_states(lin_keys, lin_values, log_decay.T, place, group)
    messages = exchange_in_group(messages, group)
    inside = intra(lin_queries, lin_keys, lin_values, running)
    if len(parts) > 1:
        outgoing += pack(spots, cache_keys, cache_values, widths[0], widths[1:])
        inside, my_owners, my_counts, messages[1], *outgoing[1:] = tied(
            (inside, my_owners, my_counts, messages[1], *outgoing[1:])
        )
    total = walk(total_kernel, messages, (), place, per)
    earlier, total = from_partners(total, places, per, group)
    def attend(i, so_far, skip=0, number=None):
        return soft_part(
            my_owners,
            my_counts,
            soft_queries,
            slab_keys,
            slab_values,
            arrived[i],
            skip,
            number or parts[i] - skip,
            sum(parts[:i]) + skip,
            chosen,
            so_far,
        )

    if len(parts) > 1:
        arrived[0], total = tied((arrived[0], total))
        early = attend(0, None, number=1)
        block, early, *earlier = tied((outgoing[1], early, *earlier))
        arrived.append(lax.all_to_all(block, "ctx", 0, 0, tiled=True))
    states = exchange_in_group(walk(enter_kernel, messages, earlier, places, per), group)

    soft_out = None
    if len(parts) > 1:
        soft_out = early if parts[0] == 1 else attend(0, early, skip=1)
        soft_out, running, states, *outgoing[2:] = tied(
            (soft_out, running, states, *outgoing[2:])
        )
        for block in outgoing[2:]:
            block, arrived[-1] = tied((block, arrived[-1]))
            arrived.append(lax.all_to_all(block, "ctx", 0, 0, tiled=True))
    attn, squares = join(lin_queries, inside, running, states, place)
    summands = [squares]
    reach = 1
    while reach < head_devices:
        if len(summands) > 1:
            summands = [summands[0] + summands[1]]
        summands.append(
            lax.ppermute(summands[0], "head", [(i, i ^ reach) for i in range(head_devices)])
        )
        reach *= 2
    features = head_devices * heads * HD
    lin_out = gated(attn, lin_gate, norm_gain, summands, features)
    for i in range(min(1, len(parts) - 1), len(parts) - 1):
        soft_out = attend(i, soft_out)
    if len(parts) > 1:
        lin_out, my_owners = tied((lin_out, my_owners))
    return (lin_out, attend(len(parts) - 1, soft_out))


def solution(mesh):
    in_specs = (
        P("ctx", "head"),
        P("ctx", "head"),
        P("ctx", "head"),
        P("ctx", "head"),
        P("ctx", "head"),
        P("head"),
        P("ctx", "head"),
        P("ctx", "head"),
        P("ctx", "head"),
        P("ctx", "head"),
        P("ctx", "head"),
        P(),
        P(),
    )
    out_specs = (P("ctx", "head"), P("ctx", "head"))
    return jax.shard_map(local, mesh=mesh, in_specs=in_specs, out_specs=out_specs, check_vma=False)
```

```python
import functools
import math

import jax
import jax.numpy as jnp
from jax import lax
from jax.experimental import pallas as pl
from jax.experimental.pallas import tpu as pltpu
from jax.sharding import PartitionSpec as P

HD = 128
BLOCK = 128
STEP_HEADS = 8
GROUP = 4
VMEM_LIMIT = 28 * 1024 * 1024
IN_VMEM = pl.BlockSpec(memory_space=pltpu.VMEM)
F32 = jnp.float32
BF16 = jnp.bfloat16
NT = (((1,), (1,)), ((), ()))
NN = (((1,), (0,)), ((), ()))


def tail_rows(per):
    return -(-3 * per // 16) * 16


def split_logs(logs):
    high = logs.astype(BF16).astype(F32)
    middle = (logs - high).astype(BF16).astype(F32)
    rows = [high, middle, logs - high - middle]
    spare = tail_rows(logs.shape[0]) - 3 * logs.shape[0]
    if spare:
        rows.append(jnp.zeros((spare, HD), F32))
    return jnp.concatenate(rows, axis=0).astype(BF16)


def params(limit=VMEM_LIMIT):
    return pltpu.CompilerParams(vmem_limit_bytes=limit)


def cost(microseconds):
    return pl.CostEstimate(
        flops=0, bytes_accessed=int(microseconds * 3.69e6), transcendentals=0
    )


def silu(u):
    half = u.astype(F32) * 0.5
    return (half + half * jnp.tanh(half)).astype(BF16)


def pack_kernel(first, spots, keys, values, *outs):
    n = outs[0].shape[0]
    per = spots.shape[0] // n
    for dest in range(n):
        spot = functools.reduce(jnp.maximum, [spots[dest * per + i] for i in range(per)])
        rows = pl.ds(pl.multiple_of(spot * BLOCK, BLOCK), BLOCK)
        start = first
        for out in outs:
            columns = slice(start, start + out.shape[3])
            out[dest, 0] = keys[rows, columns]
            out[dest, 1] = values[rows, columns]
            start += out.shape[3]


def pack(spots, n, keys, values, first, widths):
    span, column = keys.shape[1], 0
    if first % sum(widths) == 0:
        span, column, first = sum(widths), first // sum(widths), 0
    whole = pl.BlockSpec((keys.shape[0], span), lambda i, _: (0, column))
    return pl.pallas_call(
        functools.partial(pack_kernel, first),
        out_shape=[jax.ShapeDtypeStruct((n, 2, BLOCK, width), BF16) for width in widths],
        grid_spec=pltpu.PrefetchScalarGridSpec(
            num_scalar_prefetch=1,
            grid=(1,),
            in_specs=[whole, whole],
            out_specs=[IN_VMEM] * len(widths),
        ),
        compiler_params=params(50 * 1024 * 1024),
        cost_estimate=cost(4),
        name="pack",
    )(spots, keys, values)


def state_kernel(group, place, keys, values, decay, running_out, *rest):
    outs, running, hold = rest[:group], rest[group], rest[group + 1]
    step = pl.program_id(0)
    rows = keys.shape[0]
    mine = place[0]
    per = running.shape[0] // group

    @pl.when(step == 0)
    def _():
        s = lax.broadcasted_iota(jnp.int32, (rows, rows), 0)
        t = lax.broadcasted_iota(jnp.int32, (rows, rows), 1)
        running[...] = lax.dot_general(
            decay[...],
            (s <= t).astype(F32),
            NN,
            precision=lax.Precision.HIGHEST,
            preferred_element_type=F32,
        )

    here = running[pl.ds(pl.multiple_of(step * STEP_HEADS, STEP_HEADS), STEP_HEADS), :]
    running_out[...] = here
    total = here[:, rows - 1 : rows]
    fade = jnp.exp(total - here)
    logs = jnp.broadcast_to(total, (STEP_HEADS, HD))
    for dest in range(STEP_HEADS // per):
        slot = (step * (STEP_HEADS // per) + dest) ^ mine
        for i in range(per):
            head = dest * per + i
            columns = slice(head * HD, (head + 1) * HD)
            act = silu(keys[:, columns]).T
            state = jnp.dot(
                (act.astype(F32) * fade[head : head + 1, :]).astype(BF16),
                values[:, columns],
                preferred_element_type=F32,
            )
            hold[slot, i * HD : (i + 1) * HD, :] = state.astype(BF16)
        hold[slot, per * HD :, :] = split_logs(logs[dest * per : (dest + 1) * per])

    @pl.when(step == pl.num_programs(0) - 1)
    def _():
        for k, out in enumerate(outs):
            out[...] = hold[k]


def segment_states(keys, values, decay, place, group):
    heads, rows = decay.shape
    per = heads // group
    size = per * HD + tail_rows(per)
    wide = STEP_HEADS * HD
    return pl.pallas_call(
        functools.partial(state_kernel, group),
        out_shape=[jax.ShapeDtypeStruct((heads, rows), F32)]
        + [jax.ShapeDtypeStruct((size, HD), BF16)] * group,
        grid_spec=pltpu.PrefetchScalarGridSpec(
            num_scalar_prefetch=1,
            grid=(heads // STEP_HEADS,),
            in_specs=[
                pl.BlockSpec((rows, wide), lambda i, _: (0, i)),
                pl.BlockSpec((rows, wide), lambda i, _: (0, i)),
                pl.BlockSpec((heads, rows), lambda i, _: (0, 0)),
            ],
            out_specs=[pl.BlockSpec((STEP_HEADS, rows), lambda i, _: (i, 0))]
            + [pl.BlockSpec((size, HD), lambda i, _: (0, 0))] * group,
            scratch_shapes=[pltpu.VMEM((heads, rows), F32), pltpu.VMEM((group, size, HD), BF16)],
        ),
        compiler_params=params(),
        cost_estimate=cost(6),
        name="segment_states",
    )(place, keys, values, decay)


def intra_kernel(queries, keys, values, running, out):
    rows = queries.shape[0]
    column = running[...].T
    t = lax.broadcasted_iota(jnp.int32, (BLOCK, BLOCK), 0)
    s = lax.broadcasted_iota(jnp.int32, (BLOCK, BLOCK), 1)
    causal = s <= t
    for head in range(STEP_HEADS):
        columns = slice(head * HD, (head + 1) * HD)
        act_q = silu(queries[:, columns])
        act_k = silu(keys[:, columns])
        v = values[:, columns]
        for a in range(rows // BLOCK):
            mine = slice(a * BLOCK, (a + 1) * BLOCK)
            seen = (a + 1) * BLOCK
            scores = lax.dot_general(act_q[mine], act_k[:seen], NT, preferred_element_type=F32)
            gaps = column[mine, head : head + 1] - running[head : head + 1, :seen]
            pieces = []
            for b in range(a + 1):
                part = slice(b * BLOCK, (b + 1) * BLOCK)
                gap = jnp.minimum(gaps[:, part], 0.0)
                if b == a:
                    gap = jnp.where(causal, gap, -1e30)
                pieces.append((scores[:, part] * jnp.exp(gap)).astype(BF16))
            weights = pieces[0] if a == 0 else jnp.concatenate(pieces, axis=1)
            out[mine, columns] = jnp.dot(weights, v[:seen], preferred_element_type=F32)


def intra(queries, keys, values, running):
    rows, features = queries.shape
    wide = STEP_HEADS * HD
    block = pl.BlockSpec((rows, wide), lambda i: (0, i))
    return pl.pallas_call(
        intra_kernel,
        out_shape=jax.ShapeDtypeStruct((rows, features), F32),
        grid=(features // wide,),
        in_specs=[block, block, block, pl.BlockSpec((STEP_HEADS, rows), lambda i: (i, 0))],
        out_specs=block,
        compiler_params=params(),
        cost_estimate=cost(10),
        name="intra",
    )(queries, keys, values, running)


def read_logs(message, per):
    tail = message[per * HD :, :].astype(F32)
    return tail[:per] + tail[per : 2 * per] + tail[2 * per : 3 * per]


def total_kernel(group, per, place, *refs):
    arrived, out, hold = refs[:group], refs[group], refs[group + 1]
    for k in range(group):
        hold[place[0] ^ k] = arrived[k][...]
    logs = [read_logs(hold.at[j], per) for j in range(group)]
    fades = [jnp.exp(log) for log in logs]
    for head in range(per):
        rows = slice(head * HD, (head + 1) * HD)
        state = hold[0, rows, :].astype(F32)
        for j in range(1, group):
            state = fades[j][head : head + 1, :] * state + hold[j, rows, :].astype(F32)
        out[rows, :] = state.astype(BF16)
    out[per * HD :, :] = split_logs(functools.reduce(lambda x, y: x + y, logs))


def merge_kernel(group, per, bit, place, mine, partner, out):
    later = (place[1] >> bit) % 2 == 1
    logs = [read_logs(mine, per), read_logs(partner, per)]
    fade = jnp.exp(jnp.where(later, logs[0], logs[1]))
    for head in range(per):
        rows = slice(head * HD, (head + 1) * HD)
        own, other = mine[rows, :].astype(F32), partner[rows, :].astype(F32)
        first, second = jnp.where(later, other, own), jnp.where(later, own, other)
        out[rows, :] = (fade[head : head + 1, :] * first + second).astype(BF16)
    out[per * HD :, :] = split_logs(logs[0] + logs[1])


def enter_kernel(group, per, place, *refs):
    arrived, partners, refs = refs[:group], refs[group : -group - 1], refs[-group - 1 :]
    outs, hold = refs[:-1], refs[-1]
    for k in range(group):
        hold[place[0] ^ k] = arrived[k][...]
    fades = [jnp.exp(read_logs(hold.at[j], per)) for j in range(group)]
    before = [(place[1] >> bit) % 2 == 1 for bit in range(len(partners))]
    passed, log = [], jnp.zeros((per, HD), F32)
    for bit, partner in enumerate(partners):
        passed.append(jnp.exp(log))
        log = log + jnp.where(before[bit], read_logs(partner, per), 0.0)
    for head in range(per):
        rows = slice(head * HD, (head + 1) * HD)
        state = jnp.zeros((HD, HD), F32)
        for bit, partner in enumerate(partners):
            more = passed[bit][head : head + 1, :] * partner[rows, :].astype(F32)
            state = state + jnp.where(before[bit], more, 0.0)
        for j in range(group):
            own = hold[j, rows, :].astype(F32)
            hold[j, rows, :] = state.astype(BF16)
            state = fades[j][head : head + 1, :] * state + own
    for k in range(group):
        outs[k][...] = hold[place[0] ^ k, : per * HD, :]


def walk(kernel, arrived, partners, place, per):
    group = len(arrived)
    size = arrived[0].shape[0]
    out_shape, out_specs = jax.ShapeDtypeStruct((size, HD), BF16), IN_VMEM
    if kernel is enter_kernel:
        out_shape = [jax.ShapeDtypeStruct((per * HD, HD), BF16)] * group
        out_specs = [IN_VMEM] * group
    return pl.pallas_call(
        functools.partial(kernel, group, per),
        out_shape=out_shape,
        grid_spec=pltpu.PrefetchScalarGridSpec(
            num_scalar_prefetch=1,
            grid=(1,),
            in_specs=[IN_VMEM] * (group + len(partners)),
            out_specs=out_specs,
            scratch_shapes=[pltpu.VMEM((group, size, HD), BF16)],
        ),
        compiler_params=params(),
        cost_estimate=cost(2.5),
        name="walk_states",
    )(place, *arrived, *partners)


def join_kernel(group, place, queries, inside, running, *refs):
    states, (out, squares), (hold, total) = refs[:group], refs[group : group + 2], refs[group + 2 :]
    step = pl.program_id(0)
    mine = place[0]
    per = hold.shape[1] // HD

    @pl.when(step == 0)
    def _():
        for k in range(group):
            hold[mine ^ k] = states[k][...]
        total[...] = jnp.zeros_like(total)

    grow = jnp.exp(running[...].T)
    summed = jnp.zeros(total.shape, F32)
    for head in range(STEP_HEADS):
        columns = slice(head * HD, (head + 1) * HD)
        owner = step * (STEP_HEADS // per) + head // per
        part = (head % per) * HD
        passed = jnp.dot(
            silu(queries[:, columns]), hold[owner, part : part + HD, :], preferred_element_type=F32
        )
        attn = inside[:, columns] + grow[:, head : head + 1] * passed
        out[:, columns] = attn
        summed += attn * attn
    total[...] += summed

    @pl.when(step == pl.num_programs(0) - 1)
    def _():
        squares[...] = lax.dot_general(
            jnp.ones((8, HD), F32),
            total[...],
            NT,
            precision=lax.Precision.HIGHEST,
            preferred_element_type=F32,
        )


def join(queries, inside, running, states, place):
    rows, features = queries.shape
    wide = STEP_HEADS * HD
    block = pl.BlockSpec((rows, wide), lambda i, _: (0, i))
    group = len(states)
    return pl.pallas_call(
        functools.partial(join_kernel, group),
        out_shape=[
            jax.ShapeDtypeStruct((rows, features), F32),
            jax.ShapeDtypeStruct((8, rows), F32),
        ],
        grid_spec=pltpu.PrefetchScalarGridSpec(
            num_scalar_prefetch=1,
            grid=(features // wide,),
            in_specs=[block, block, pl.BlockSpec((STEP_HEADS, rows), lambda i, _: (i, 0))]
            + [IN_VMEM] * group,
            out_specs=[block, pl.BlockSpec((8, rows), lambda i, _: (0, 0))],
            scratch_shapes=[
                pltpu.VMEM((group,) + states[0].shape, BF16),
                pltpu.VMEM((rows, HD), F32),
            ],
        ),
        compiler_params=params(),
        cost_estimate=cost(7),
        name="join_states",
    )(place, queries, inside, running, *states)


def gate_kernel(features, attn, gate, gain, *refs):
    out = refs[-1]
    squares = refs[0][...]
    for more in refs[1:-1]:
        squares = squares + more[...]
    scaling = lax.rsqrt(squares / features + 1e-06).T[:, :1]
    half = gate[...].astype(F32) * 0.5
    opened = 0.5 + 0.5 * jnp.tanh(half)
    out[...] = (attn[...] * scaling * gain[...] * opened).astype(BF16)


def gated(attn, gate, gain, squares, features):
    rows, here = attn.shape
    wide = STEP_HEADS * HD
    block = pl.BlockSpec((rows, wide), lambda i: (0, i))
    return pl.pallas_call(
        functools.partial(gate_kernel, features),
        out_shape=jax.ShapeDtypeStruct((rows, here), BF16),
        grid=(here // wide,),
        in_specs=[block, block, pl.BlockSpec((1, wide), lambda i: (0, i))]
        + [IN_VMEM] * len(squares),
        out_specs=block,
        compiler_params=params(),
        cost_estimate=cost(6),
        name="gated_norm",
    )(attn, gate, gain.reshape(1, here), *squares)


def exchange_in_group(messages, group):
    n = lax.axis_size("ctx")
    return [messages[0]] + [
        lax.ppermute(messages[k], "ctx", [(i, i ^ k) for i in range(n)]) for k in range(1, group)
    ]


def merge(total, partner, place, per, group, bit):
    return pl.pallas_call(
        functools.partial(merge_kernel, group, per, bit),
        out_shape=jax.ShapeDtypeStruct(total.shape, BF16),
        grid_spec=pltpu.PrefetchScalarGridSpec(
            num_scalar_prefetch=1,
            grid=(1,),
            in_specs=[IN_VMEM, IN_VMEM],
            out_specs=IN_VMEM,
        ),
        compiler_params=params(),
        cost_estimate=cost(2),
        name="merge_states",
    )(place, total, partner)


def from_partners(total, place, per, group):
    n = lax.axis_size("ctx")
    partners = []
    reach = group
    while reach < n:
        if partners:
            total = merge(total, partners[-1], place, per, group, len(partners) - 1)
        partners.append(lax.ppermute(total, "ctx", [(i, i ^ reach) for i in range(n)]))
        reach *= 2
    return partners, total


def soft_kernel(chosen, skip, first, wide, owners, counts, queries, slab_k, slab_v, arrived, *refs):
    out, top, weight_sum, mixed = refs[-4:]
    b = pl.program_id(1)
    count = counts[b]
    columns = pl.ds(pl.multiple_of((skip + pl.program_id(0)) * HD, HD), HD)
    own = pl.ds(pl.multiple_of((first + pl.program_id(0)) * HD, HD), HD)
    mine = pl.ds(pl.multiple_of(b * BLOCK, BLOCK), BLOCK)
    heads = wide // HD
    rows = min(4, heads) * BLOCK
    chunks = heads * BLOCK // rows
    scale = math.log2(math.e) / math.sqrt(HD)

    def spans():
        return [(r, slice(r * rows, (r + 1) * rows)) for r in range(chunks)]

    def queries_of(r):
        per = rows // BLOCK
        start = (first + pl.program_id(0)) * wide + per * r * HD
        parts = [
            queries[mine, pl.ds(pl.multiple_of(start + i * HD, HD), HD)] for i in range(per)
        ]
        return jnp.concatenate(parts, axis=0)

    def fetch(kind, first, number):
        parts = [
            arrived[owners[b * chosen + first + i], kind, :, columns] for i in range(number)
        ]
        return parts[0] if number == 1 else jnp.concatenate(parts, axis=0)

    def weigh(scores, highest):
        number = scores.shape[1] // BLOCK
        parts = [
            jnp.exp2(scores[:, i * BLOCK : (i + 1) * BLOCK] * scale - highest)
            for i in range(number)
        ]
        summed = functools.reduce(lambda x, y: x + y, parts)
        parts = [part.astype(BF16) for part in parts]
        return summed, parts[0] if number == 1 else jnp.concatenate(parts, axis=1)

    def cached(first, number):
        k, v = fetch(0, first, number), fetch(1, first, number)
        for r, at in spans():
            scores = lax.dot_general(queries_of(r), k, NT, preferred_element_type=F32)
            summed, w = weigh(scores, top[at, :])
            weight_sum[at, :] += summed
            mixed[at, :] += jnp.dot(w, v, preferred_element_type=F32)

    def raise_top(j):
        k = fetch(0, j, 1)
        for r, at in spans():
            scores = lax.dot_general(queries_of(r), k, NT, preferred_element_type=F32)
            here = jnp.max(scores, axis=1, keepdims=True) * scale
            top[at, :] = jnp.maximum(top[at, :], here)

    def attempt(again):
        def slab(seen):
            t = lax.broadcasted_iota(jnp.int32, (rows, seen), 0) % BLOCK
            s_at = lax.broadcasted_iota(jnp.int32, (rows, seen), 1)
            causal = s_at <= t + b * BLOCK
            k, v = slab_k[:seen, own], slab_v[:seen, own]
            for r, at in spans():
                scores = lax.dot_general(queries_of(r), k, NT, preferred_element_type=F32)
                scores = jnp.where(causal, scores, -1e30)
                highest = jnp.max(scores, axis=1, keepdims=True) * scale
                top[at, :] = jnp.maximum(top[at, :], highest)
                summed, w = weigh(scores, top[at, :])
                weight_sum[at, :] = summed
                mixed[at, :] = jnp.dot(w, v, preferred_element_type=F32)

        @pl.when(b == 0)
        def _():
            slab(BLOCK)

        @pl.when(b > 0)
        def _():
            slab(slab_k.shape[0])

        def eight(p, carry):
            cached(8 * p, 8)
            return carry

        lax.fori_loop(0, count // 8, eight, 0)
        for number in (4, 2, 1):

            @pl.when((count // number) % 2 == 1)
            def _(number=number):
                cached((count // (2 * number)) * (2 * number), number)

        fine = jnp.max(weight_sum[...]) < 1e25

        @pl.when(jnp.logical_not(fine))
        def _():
            def turn(j, carry):
                raise_top(j)
                return carry

            lax.fori_loop(0, count, turn, 0)

        return jnp.logical_not(fine)

    top[...] = jnp.full(top.shape, -1e30, F32)
    lax.while_loop(lambda again: again, attempt, jnp.bool_(True))
    for head in range(heads):
        at = slice(head * BLOCK, (head + 1) * BLOCK)
        total = jnp.sum(weight_sum[at, :], axis=1, keepdims=True)
        out[:, head * HD : (head + 1) * HD] = (mixed[at, :] / total).astype(BF16)


def soft_part(owners, counts, queries, slab_k, slab_v, arrived, skip, kv_here, first, chosen, so_far):
    rows, features = queries.shape
    wide = features // (slab_k.shape[1] // HD)
    blocks = rows // BLOCK
    grid_spec = pltpu.PrefetchScalarGridSpec(
        num_scalar_prefetch=2,
        grid=(kv_here, blocks),
        in_specs=[
            IN_VMEM,
            IN_VMEM,
            IN_VMEM,
            IN_VMEM,
        ]
        + ([] if so_far is None else [pl.BlockSpec(memory_space=pl.ANY)]),
        out_specs=pl.BlockSpec((BLOCK, wide), lambda h, b, *_: (b, first + h)),
        scratch_shapes=[
            pltpu.VMEM((wide // HD * BLOCK, BLOCK), F32),
            pltpu.VMEM((wide // HD * BLOCK, BLOCK), F32),
            pltpu.VMEM((wide // HD * BLOCK, BLOCK), F32),
        ],
    )
    return pl.pallas_call(
        functools.partial(soft_kernel, chosen, skip, first, wide),
        out_shape=jax.ShapeDtypeStruct((rows, features), BF16),
        grid_spec=grid_spec,
        input_output_aliases={} if so_far is None else {6: 0},
        compiler_params=params(),
        cost_estimate=cost(8 * kv_here),
        name="soft_attention",
    )(owners, counts, queries, slab_k, slab_v, arrived, *(() if so_far is None else (so_far,)))


def parts_of(kv_count):
    return [kv_count - kv_count // 2, kv_count // 2] if kv_count > 1 else [1]


def local(
    lin_queries,
    lin_keys,
    lin_values,
    log_decay,
    lin_gate,
    norm_gain,
    soft_queries,
    slab_keys,
    slab_values,
    cache_keys,
    cache_values,
    block_lists,
    live_counts,
):
    n = lax.axis_size("ctx")
    me = lax.axis_index("ctx")
    head_devices = lax.axis_size("head")
    heads = log_decay.shape[1]
    chosen = block_lists.shape[1]
    kv_count = cache_keys.shape[1] // HD
    stored = cache_keys.shape[0] // BLOCK
    blocks_here = block_lists.shape[0] // n
    group = 1
    while group < GROUP and 2 * group <= n and heads % (2 * group) == 0:
        group *= 2
    per = heads // group

    lists = block_lists.reshape(n, blocks_here, chosen)
    counts = live_counts.reshape(n, blocks_here)
    live = jnp.arange(chosen)[None, None, :] < counts[:, :, None]
    owner = lists // stored
    spots = jnp.max(jnp.where(live & (owner == me), lists % stored, 0), axis=2).reshape(-1)
    my_owners = lax.dynamic_slice_in_dim(owner, me, 1, 0).reshape(blocks_here * chosen)
    my_counts = lax.dynamic_slice_in_dim(counts, me, 1, 0).reshape(blocks_here)
    place = (me % group).reshape(1)
    places = jnp.stack([me % group, me // group])

    tied = lax.optimization_barrier
    parts = parts_of(kv_count)
    widths = [part * HD for part in parts]
    outgoing = list(pack(spots, n, cache_keys, cache_values, 0, widths[:1]))
    arrived = [lax.all_to_all(outgoing[0], "ctx", 0, 0, tiled=True)]

    running, *messages = segment_states(lin_keys, lin_values, log_decay.T, place, group)
    messages = exchange_in_group(messages, group)
    inside = intra(lin_queries, lin_keys, lin_values, running)
    if len(parts) > 1:
        outgoing += pack(spots, n, cache_keys, cache_values, widths[0], widths[1:])
        inside, my_owners, my_counts, messages[1], *outgoing[1:] = tied(
            (inside, my_owners, my_counts, messages[1], *outgoing[1:])
        )
    total = walk(total_kernel, messages, (), place, per)
    earlier, total = from_partners(total, places, per, group)
    def attend(i, so_far, skip=0, number=None):
        return soft_part(
            my_owners,
            my_counts,
            soft_queries,
            slab_keys,
            slab_values,
            arrived[i],
            skip,
            number or parts[i] - skip,
            sum(parts[:i]) + skip,
            chosen,
            so_far,
        )

    if len(parts) > 1:
        arrived[0], total = tied((arrived[0], total))
        early = attend(0, None, number=1)
        block, early, *earlier = tied((outgoing[1], early, *earlier))
        arrived.append(lax.all_to_all(block, "ctx", 0, 0, tiled=True))
    states = exchange_in_group(walk(enter_kernel, messages, earlier, places, per), group)

    soft_out = None
    if len(parts) > 1:
        soft_out = early if parts[0] == 1 else attend(0, early, skip=1)
        soft_out, running, states, *outgoing[2:] = tied(
            (soft_out, running, states, *outgoing[2:])
        )
        for block in outgoing[2:]:
            block, arrived[-1] = tied((block, arrived[-1]))
            arrived.append(lax.all_to_all(block, "ctx", 0, 0, tiled=True))
    attn, squares = join(lin_queries, inside, running, states, place)
    summands = [squares]
    reach = 1
    while reach < head_devices:
        if len(summands) > 1:
            summands = [summands[0] + summands[1]]
        summands.append(
            lax.ppermute(summands[0], "head", [(i, i ^ reach) for i in range(head_devices)])
        )
        reach *= 2
    features = head_devices * heads * HD
    lin_out = gated(attn, lin_gate, norm_gain, summands, features)
    for i in range(min(1, len(parts) - 1), len(parts) - 1):
        soft_out = attend(i, soft_out)
    if len(parts) > 1:
        lin_out, my_owners = tied((lin_out, my_owners))
    return (lin_out, attend(len(parts) - 1, soft_out))


def solution(mesh):
    in_specs = (
        P("ctx", "head"),
        P("ctx", "head"),
        P("ctx", "head"),
        P("ctx", "head"),
        P("ctx", "head"),
        P("head"),
        P("ctx", "head"),
        P("ctx", "head"),
        P("ctx", "head"),
        P("ctx", "head"),
        P("ctx", "head"),
        P(),
        P(),
    )
    out_specs = (P("ctx", "head"), P("ctx", "head"))
    return jax.shard_map(local, mesh=mesh, in_specs=in_specs, out_specs=out_specs, check_vma=False)
```
